128 devices in a mesh: dp: 32 (over x, z, core), help: 4 (over y).
Axes of the slice: x: 4, y: 4, z: 4, core: 2. Of those that a mesh axis runs over, the one named last changes fastest.
Arguments:
- embeddings: bfloat16 [131072, 1024], P(('dp', 'help')), may hold values from -1600 to 1600
- clusters: int32 [131072], P(('dp', 'help')), may hold values from 0 to 63, as said below
- doc_order: int32 [131072], P(('dp', 'help')), may hold values from 0 to 131071, each once
Outputs:
- similarity: float32 [131072], P(('dp', 'help'))
The draws below stay inside these ranges and needn't reach their ends.
Inputs may be any that keep to these rules, and one draw needn't show every extreme that they name: `clusters`: among the 1024 documents of one device no cluster appears more than 32 times; one cluster appears exactly 32 times on every device. `doc_order`: every number from 0 to 131071 appears once.
All inputs are finite; a program needn't handle non-finite values.
Results may differ from the reference program's by a relative error of at most 0.00033.
Values may be sent and summed in bfloat16 or wider, within the bound.
A program may use at most 128 MiB of HBM per device.

```python
import math
import jax
import jax.numpy as jnp
from jax import lax

D = 1024
ROWS_DEV = 1024
CL_DEV = 2
CLUSTERS = 64
DOCS = 131072
MEMBERS = 4096
N_DP = 32
N_HELP = 4


def cluster_plan(key):
    plan_key = jax.random.fold_in(key, 11)
    cluster_count = CL_DEV * N_DP
    slot_cap = 2 * ROWS_DEV // cluster_count
    blocks = N_DP * N_HELP
    slot_total = cluster_count * slot_cap
    splits = jax.random.split(plan_key, 5)
    levels = jax.random.randint(splits[0], (cluster_count,), 0, 4)
    jitter = jax.random.randint(splits[1], (blocks, slot_total), 0, 1024)
    slot_owner = jnp.arange(slot_total, dtype=jnp.int32) // slot_cap
    pinned = jax.random.randint(splits[2], (), 0, cluster_count)
    per_block = jax.random.randint(splits[3], (blocks,), 0, cluster_count)
    forced = (slot_owner[None, :] == pinned) | (slot_owner[None, :] == per_block[:, None])
    scores = jitter + levels[slot_owner][None, :] * 256 + forced.astype(jnp.int32) * 4096
    ranked = scores * slot_total + jnp.arange(slot_total, dtype=jnp.int32)[None, :]
    chosen = lax.top_k(ranked, ROWS_DEV)[1]

    def shuffle_one(subkey):
        return jax.random.permutation(subkey, ROWS_DEV)
    shuffle = jax.vmap(shuffle_one)(jax.random.split(splits[4], blocks))
    chosen = jnp.take_along_axis(chosen, shuffle, axis=1)
    return (chosen // slot_cap).reshape(-1).astype(jnp.int32)


def draw_clusters(key, part):
    return cluster_plan(key)


def draw_embeddings(key, part):
    cluster_ids = cluster_plan(key)
    key = jax.random.fold_in(key, 5)
    doc_count = ROWS_DEV * N_DP * N_HELP
    cluster_count = CL_DEV * N_DP
    proto_count = max(doc_count // (2 * cluster_count), 1)
    factor_count = 8
    splits = jax.random.split(key, 11)
    private = jnp.clip(jax.random.normal(splits[0], (doc_count, D), jnp.float32), -4.0, 4.0)
    prototypes = jnp.clip(jax.random.normal(splits[1], (cluster_count * proto_count, D), jnp.float32), -4.0, 4.0)
    proto_pick = cluster_ids * proto_count + jax.random.randint(splits[2], (doc_count,), 0, proto_count)
    shared = prototypes[proto_pick]
    weight_dup = jax.random.uniform(splits[3], (doc_count, 1), jnp.float32, 0.0, 3.0)
    profile = jnp.exp(jax.random.uniform(splits[4], (D,), jnp.float32, -0.69, 0.69))
    position = jnp.arange(doc_count, dtype=jnp.float32)[:, None] / doc_count
    tilt_power = jax.random.uniform(splits[5], (D,), jnp.float32, -1.0, 1.0)
    drift_factor = jnp.exp(tilt_power[None, :] * jnp.log1p(2.0 * position))
    loadings = 0.35 * jnp.clip(jax.random.normal(splits[9], (factor_count, D), jnp.float32), -3.0, 3.0)
    factor_scores = jnp.clip(jax.random.normal(splits[10], (doc_count, factor_count), jnp.float32), -3.0, 3.0)
    common_part = jnp.zeros((doc_count, D), jnp.float32)
    for factor_index in range(factor_count):
        common_part = common_part + factor_scores[:, factor_index:factor_index + 1] * loadings[factor_index][None, :]
    column = jnp.exp(jax.random.uniform(splits[6], (D,), jnp.float32, 0.0, math.log(10.0)))
    row_scale = jnp.exp(jax.random.uniform(splits[7], (doc_count, 1), jnp.float32, 0.0, math.log(4.0)))
    inner = 0.6 * (private * drift_factor + common_part + weight_dup * profile[None, :] * shared)
    values = row_scale * column[None, :] * inner
    return values.astype(jnp.bfloat16)


def setup_inputs(seed: int = 0) -> dict:
    keys = jax.random.split(jax.random.key(seed), 4)
    embeddings = draw_embeddings(jax.random.fold_in(keys[3], 71), 0)
    clusters = draw_clusters(jax.random.fold_in(keys[3], 71), 0)
    doc_order = jax.random.permutation(keys[2], DOCS).astype(jnp.int32)
    return dict(embeddings=embeddings, clusters=clusters, doc_order=doc_order)


def whitening(gram_total, col_sum, doc_count, feature_count):
    center = col_sum / doc_count
    spread = gram_total / doc_count - center[:, None] * center[None, :]
    ridge_term = 0.001 * jnp.trace(spread) / feature_count
    identity = jnp.eye(feature_count, dtype=jnp.float32)
    factor = jnp.linalg.cholesky(spread + ridge_term * identity)
    inverse = lax.linalg.triangular_solve(factor, identity, left_side=True, lower=True)
    return (center, inverse)

def whiten(source_rows, center, inverse):
    shifted = lax.dot_general(center[None, :].astype(jnp.float32), inverse.astype(jnp.float32), (((1,), (1,)), ((), ())), precision=lax.Precision.HIGHEST, preferred_element_type=jnp.float32)
    raw_rows = source_rows.astype(jnp.float32)
    projected = lax.dot_general(raw_rows.astype(jnp.float32), inverse.astype(jnp.float32), (((1,), (1,)), ((), ())), precision=lax.Precision.HIGH, preferred_element_type=jnp.float32) - shifted
    row_scale = lax.rsqrt(lax.optimization_barrier(jnp.sum(projected * projected, axis=1, keepdims=True)) + 1e-06)
    return (projected * row_scale).astype(jnp.bfloat16)

def reference(embeddings, clusters, doc_order):
    doc_count = embeddings.shape[0]
    feature_count = embeddings.shape[1]
    col_sum = lax.optimization_barrier(jnp.sum(embeddings, axis=0, dtype=jnp.float32))
    gram_total = lax.dot_general(embeddings.astype(jnp.float32), embeddings.astype(jnp.float32), (((0,), (0,)), ((), ())), preferred_element_type=jnp.float32)
    center, inverse = whitening(gram_total, col_sum, doc_count, feature_count)
    whitened = whiten(embeddings, center, inverse)
    members = clusters[:, None] == jnp.arange(CLUSTERS, dtype=jnp.int32)[None, :]
    running = jnp.cumsum(members.astype(jnp.int32), axis=0)
    rank_index = lax.optimization_barrier(jnp.sum(jnp.where(members, running - 1, 0), axis=1)).astype(jnp.int32)
    position = (clusters * MEMBERS + rank_index).astype(jnp.int32)
    padded = jnp.zeros((CLUSTERS * MEMBERS, feature_count), jnp.bfloat16).at[position].set(whitened)
    padded_order = jnp.full((CLUSTERS * MEMBERS,), doc_count, jnp.int32).at[position].set(doc_order)
    padded = padded.reshape(CLUSTERS, MEMBERS, feature_count)
    padded_order = padded_order.reshape(CLUSTERS, MEMBERS)

    def one_cluster(bundle):
        group_rows, group_order = bundle
        values = group_rows.astype(jnp.float32)
        scores = jnp.dot(values.astype(jnp.float32), values.T.astype(jnp.float32), precision=lax.Precision.HIGHEST, preferred_element_type=jnp.float32)
        earlier = group_order[None, :] < group_order[:, None]
        return lax.optimization_barrier(jnp.max(jnp.where(earlier, scores, -jnp.inf), axis=1))
    best_prior = lax.map(one_cluster, (padded, padded_order)).reshape(-1)
    return jnp.maximum(best_prior[position], -1.0)
```

```python
import jax
import jax.numpy as jnp
from jax import lax
from jax.experimental import pallas as pl
from jax.experimental.pallas import tpu as pltpu
from jax.sharding import PartitionSpec as P

F32 = jnp.float32
BF = jnp.bfloat16
MESH = pl.DeviceIdType.MESH
BL = 128
SEND = 32
CHIPS = 64
DIGITS = 128
AXES = ("x", "y", "z")


def dot(a, b, ca, cb):
    return lax.dot_general(a, b, (((ca,), (cb,)), ((), ())), preferred_element_type=F32)


def dot_full(a, b, ca, cb):
    return lax.dot_general(
        a,
        b,
        (((ca,), (cb,)), ((), ())),
        precision=lax.Precision.HIGHEST,
        preferred_element_type=F32,
    )


def bcast(v):
    return jnp.broadcast_to(v, (8, BL))


def sum_tree(x):
    while len(x) > 1:
        x = [x[i] + x[i + 1] for i in range(0, len(x), 2)]
    return x[0]


def chol_inverse_block(rows):
    sub = lax.broadcasted_iota(jnp.int32, (8, BL), 0)
    lane = lax.broadcasted_iota(jnp.int32, (8, BL), 1)
    unit = [jnp.where(lane == sub + 8 * i, 1.0, 0.0).astype(F32) for i in range(16)]
    rows = list(rows)
    out = []
    for p in range(16):
        r, t = rows[p], unit[p]
        tf = t
        cols = [bcast(r[:, 8 * p + k : 8 * p + k + 1]) for k in range(8)]
        scale = jnp.zeros((8, BL), F32)
        for j in range(8):
            d = bcast(cols[j][j : j + 1])
            inv = 1.0 / d
            pick = sub == j
            scale = jnp.where(pick, d, scale)
            cj = cols[j]
            tf = tf - jnp.where(sub > j, cj, 0.0) * (bcast(tf[j : j + 1]) * inv)
            for k in range(j + 1, 8):
                row = bcast(cols[k][j : j + 1]) * inv
                cols[k] = jnp.where(pick, row, cols[k] - cj * row)
            row = bcast(r[j : j + 1]) * inv
            r = jnp.where(pick, row, r - cj * row)
            row = bcast(t[j : j + 1]) * inv
            t = jnp.where(pick, row, t - cj * row)
        out.append(tf * lax.rsqrt(scale))
        for i in range(p + 1, 16):
            m = [bcast(rows[i][:, 8 * p + k : 8 * p + k + 1]) for k in range(8)]
            rows[i] = rows[i] - sum_tree([m[k] * bcast(r[k : k + 1]) for k in range(8)])
            unit[i] = unit[i] - sum_tree([m[k] * bcast(t[k : k + 1]) for k in range(8)])
    return out


def factor(m_ref, w_ref):
    blocks = m_ref.shape[0] // BL

    def step(p, _):
        off = pl.multiple_of(p * BL, BL)
        here = pl.ds(off, BL)
        out = chol_inverse_block([m_ref[pl.ds(off + 8 * i, 8), here] for i in range(16)])
        for i in range(16):
            w_ref[8 * i : 8 * i + 8, :] = out[i]
        w = w_ref[...]
        m_ref[here, :] = dot_full(w, m_ref[here, :], 1, 0)
        m_ref[here, here] = w

        def trail(i, _):
            there = pl.ds(pl.multiple_of(i * BL, BL), BL)
            g = m_ref[here, there]
            m_ref[there, here] = jnp.zeros((BL, BL), F32)
            m_ref[there, :] = m_ref[there, :] - dot_full(g, m_ref[here, :], 0, 0)
            return 0

        lax.fori_loop(p + 1, blocks, trail, 0)
        return 0

    lax.fori_loop(0, blocks, step, 0)


def place(i):
    return min(i, 7 - i) * BL, 0 if i < 4 else (i + 1) * BL


def slots_of(clusters_row):
    n = clusters_row.shape[1]
    member = lax.broadcasted_iota(jnp.int32, (CHIPS, n), 0) == clusters_row
    before = lax.broadcasted_iota(jnp.int32, (n, n), 0) < lax.broadcasted_iota(jnp.int32, (n, n), 1)
    count = dot(member.astype(F32).astype(BF), before.astype(F32).astype(BF), 1, 0)
    slot = jnp.sum(jnp.where(member, count, 0.0), axis=0, keepdims=True)
    return member, slot.astype(jnp.int32)


def digits_of(order_row, doc_count):
    n = order_row.shape[1]
    value = doc_count - order_row
    row = lax.broadcasted_iota(jnp.int32, (DIGITS, n), 0)
    d = jnp.where(row == 0, value >> 16, jnp.where(row == 1, (value >> 8) & 255, value & 255))
    return jnp.where(row < 3, d, 0).astype(F32).T.astype(BF)


def kernel(
    doc_count,
    emb_ref,
    clusters_ref,
    order_ref,
    out_ref,
    emb,
    outgoing,
    received,
    keys,
    packed,
    half_in,
    acc,
    in1,
    sum1,
    in2,
    in3,
    total,
    mat,
    w_block,
    w_hi,
    w_lo,
    key_rank,
    ret_out,
    ret_in,
    emb_sem,
    core_send,
    core_recv,
    ring_send,
    ring_recv,
    up_send,
    up_recv,
    out_send,
    out_recv,
    pair_send,
    pair_recv,
    ret_send,
    ret_recv,
):
    dp = lax.axis_index("dp")
    y = lax.axis_index("help")
    core = dp % 2
    x = dp // 8
    z = (dp // 2) % 4
    chip = (dp // 2) * 4 + y
    sibling = (dp + 1 - 2 * core, y)
    rows = emb.shape[0]
    width = emb.shape[1]

    def chip_device(c):
        return ((c // 4) * 2 + core, c % 4)

    def axis_peer(axis, d):
        if axis == "x":
            to = (x + d) % 4
            return ((to * 4 + z) * 2 + core, y), to
        if axis == "z":
            to = (z + d) % 4
            return ((x * 4 + to) * 2 + core, y), to
        to = (y + d) % 4
        return (dp, to), to

    place_on = {"x": x, "y": y, "z": z}

    barrier = pltpu.get_barrier_semaphore()

    def greet(d, _):
        pl.semaphore_signal(
            barrier, inc=1, device_id=chip_device((chip + d) % CHIPS), device_id_type=MESH
        )
        return 0

    lax.fori_loop(1, CHIPS, greet, 0)
    pl.semaphore_signal(barrier, inc=1, device_id=sibling, device_id_type=MESH)
    load = pltpu.make_async_copy(emb_ref, emb, emb_sem)
    load.start()
    member, slot = slots_of(clusters_ref[...])
    target = clusters_ref[...] * SEND + slot
    digits = digits_of(order_ref[...], doc_count)
    load.wait()

    col_sum = dot(jnp.ones((8, rows), BF), emb[...], 1, 0)
    sub = lax.broadcasted_iota(jnp.int32, (BL, BL), 0)
    lane = lax.broadcasted_iota(jnp.int32, (BL, BL), 1)
    for b in range(width // 256):
        block = dot(emb[:, 256 * b : 256 * b + 256], emb[:, 256 * b :], 0, 0)
        for i in (2 * b, 2 * b + 1):
            r0, c0 = place(i)
            skip = (i - 2 * b) * BL
            part = block[skip : skip + BL, skip:]
            w = part.shape[1]
            packed[r0 : r0 + BL, c0 : c0 + w] = part
            cs = jnp.broadcast_to(col_sum[0:1, i * BL : i * BL + BL], (BL, BL))
            spare = jnp.where(sub == BL - 2, cs, pltpu.roll(cs, 64, 1))
            use = (sub >= BL - 2) & (lane < 64)
            packed[r0 : r0 + BL, c0 : c0 + BL] = jnp.where(use, spare, part[:, :BL])

    pl.semaphore_wait(barrier, CHIPS)

    half = packed.shape[0] // 2
    mine = pl.ds(pl.multiple_of(core * half, 8), half)
    other = pl.ds(pl.multiple_of((1 - core) * half, 8), half)
    swap = pltpu.make_async_remote_copy(
        src_ref=packed.at[other],
        dst_ref=half_in,
        send_sem=core_send,
        recv_sem=core_recv,
        device_id=sibling,
        device_id_type=MESH,
    )
    swap.start()

    def place_rows(k, _):
        b = (k + chip // 8) % 8
        first = pl.multiple_of(b * 256, 256)
        here = lax.broadcasted_iota(jnp.int32, (256, rows), 0) + first
        pick = (here == target).astype(F32).astype(BF)
        outgoing[pl.ds(first, 256), 0:width] = dot(pick, emb[...], 1, 0).astype(BF)
        outgoing[pl.ds(first, 256), width:] = dot(pick, digits, 1, 0).astype(BF)
        return 0

    lax.fori_loop(0, 8, place_rows, 0)
    swap.wait_recv()
    acc[...] = packed[mine, :] + half_in[...]

    def ring_copy(stage, q, d, src, dst, device):
        return pltpu.make_async_remote_copy(
            src_ref=src,
            dst_ref=dst,
            send_sem=ring_send.at[stage * 9 + q * 3 + d - 1],
            recv_sem=ring_recv.at[stage * 9 + q * 3 + d - 1],
            device_id=device,
            device_id_type=MESH,
        )

    third = acc.shape[1] // 3
    cols = [slice(q * third, (q + 1) * third) for q in range(3)]
    axis_a = [AXES[q] for q in range(3)]
    axis_b = [AXES[(q + 1) % 3] for q in range(3)]
    axis_c = [AXES[(q + 2) % 3] for q in range(3)]
    sent = []
    stage1 = {}
    for d in (2, 1, 3):
        for q in range(3):
            device, to = axis_peer(axis_a[q], d)
            src = acc.at[pl.ds(pl.multiple_of(to * 64, 64), 64), cols[q]]
            c = ring_copy(0, q, d, src, in1.at[q, d - 1], device)
            c.start()
            stage1[q, d] = c
    stage2 = {}
    for q in range(3):
        for d in (1, 3, 2):
            stage1[q, d].wait_recv()
        a = place_on[axis_a[q]]
        own = acc[pl.ds(pl.multiple_of(a * 64, 64), 64), cols[q]]
        sum1[q] = (own + in1[q, 0]) + (in1[q, 1] + in1[q, 2])
        for d in (2, 1, 3):
            device, to = axis_peer(axis_b[q], d)
            src = sum1.at[q, pl.ds(pl.multiple_of(to * 16, 16), 16), :]
            c = ring_copy(1, q, d, src, in2.at[q, d - 1], device)
            c.start()
            stage2[q, d] = c
    stage3 = {}
    for q in range(3):
        for d in (1, 3, 2):
            stage2[q, d].wait_recv()
        b = place_on[axis_b[q]]
        c_at = place_on[axis_c[q]]
        own = sum1[q, pl.ds(pl.multiple_of(b * 16, 16), 16), :]
        in3[q, c_at] = (own + in2[q, 0]) + (in2[q, 1] + in2[q, 2])
        for d in (2, 1, 3):
            device, to = axis_peer(axis_c[q], d)
            c = ring_copy(2, q, d, in3.at[q, c_at], in3.at[q, c_at], device)
            c.start()
            stage3[q, d] = c
    stage4 = {}
    for q in range(3):
        for d in (1, 3, 2):
            stage3[q, d].wait_recv()
        a, b = place_on[axis_a[q]], place_on[axis_b[q]]
        there = pl.ds(pl.multiple_of(core * half + a * 64 + b * 16, 16), 16)
        total[there, cols[q]] = (in3[q, 0] + in3[q, 1]) + (in3[q, 2] + in3[q, 3])
        for d in (2, 1, 3):
            device, to = axis_peer(axis_b[q], d)
            c = ring_copy(3, q, d, total.at[there, cols[q]], total.at[there, cols[q]], device)
            c.start()
            stage4[q, d] = c
    stage5 = {}
    for q in range(3):
        for d in (1, 3, 2):
            stage4[q, d].wait_recv()
        a = place_on[axis_a[q]]
        there = pl.ds(pl.multiple_of(core * half + a * 64, 64), 64)
        for d in (2, 1, 3):
            device, to = axis_peer(axis_a[q], d)
            c = ring_copy(4, q, d, total.at[there, cols[q]], total.at[there, cols[q]], device)
            c.start()
            stage5[q, d] = c
    up = []
    for q in range(3):
        for d in (1, 3, 2):
            stage5[q, d].wait_recv()
        c = pltpu.make_async_remote_copy(
            src_ref=total.at[mine, cols[q]],
            dst_ref=total.at[mine, cols[q]],
            send_sem=up_send.at[q],
            recv_sem=up_recv.at[q],
            device_id=sibling,
            device_id_type=MESH,
        )
        c.start()
        up.append(c)

    def out_copy(to, at, source):
        return pltpu.make_async_remote_copy(
            src_ref=outgoing.at[pl.ds(pl.multiple_of(to * SEND, SEND), SEND), :],
            dst_ref=received.at[pl.ds(pl.multiple_of(source * SEND, SEND), SEND), :],
            send_sem=out_send.at[at],
            recv_sem=out_recv.at[at],
            device_id=chip_device(to),
            device_id_type=MESH,
        )

    def send_out(d, _):
        out_copy((chip + d) % CHIPS, d, chip).start()
        return 0

    lax.fori_loop(1, CHIPS, send_out, 0)
    own_rows = pl.ds(pl.multiple_of(chip * SEND, SEND), SEND)
    received[own_rows, :] = outgoing[own_rows, :]
    for c in up:
        c.wait_recv()

    inv_n = 1.0 / doc_count
    center = []
    trace = jnp.zeros((BL, BL), F32)
    for i in range(8):
        r0, c0 = place(i)
        d = total[r0 : r0 + BL, c0 : c0 + BL]
        tail = d[BL - 8 :, :]
        c = jnp.where(lane[:1] < 64, tail[6:7], pltpu.roll(tail, 64, 1)[7:8]) * inv_n
        center.append(c)
        cb = jnp.broadcast_to(c, (BL, BL))
        trace = trace + jnp.where(lane == sub, d * inv_n - cb * cb, 0.0)
    trace = jnp.sum(jnp.sum(trace, axis=1, keepdims=True), axis=0, keepdims=True)
    ridge = 0.001 * trace * (1.0 / width)
    for i in range(8):
        r0, c0 = place(i)
        col = jnp.broadcast_to(center[i], (BL, BL)).T
        for j in range(i, 8):
            g = total[r0 : r0 + BL, c0 + (j - i) * BL : c0 + (j - i + 1) * BL]
            if j == i:
                g = jnp.where(lane >= sub, g, g.T)
            v = g * inv_n - col * center[j]
            if j == i:
                v = v + jnp.where(lane == sub, ridge, 0.0)
            mat[i * BL : (i + 1) * BL, j * BL : (j + 1) * BL] = v
        for j in range(i):
            mat[i * BL : (i + 1) * BL, j * BL : (j + 1) * BL] = jnp.zeros((BL, BL), F32)
    factor(mat, w_block)
    shift = []
    for j in range(8):
        shift.append(
            dot_full(
                jnp.concatenate([jnp.broadcast_to(c, (8, BL)) for c in center[: j + 1]], axis=1),
                mat[j * BL : (j + 1) * BL, : (j + 1) * BL],
                1,
                1,
            )[0:1]
        )
    shift = jnp.concatenate(shift, axis=1)
    for i in range(8):
        for j in range(8):
            at = (slice(i * BL, (i + 1) * BL), slice(j * BL, (j + 1) * BL))
            if j <= i:
                v = mat[at]
                hi = v.astype(BF)
                w_hi[at] = hi
                w_lo[at] = (v - hi.astype(F32)).astype(BF)
            else:
                w_hi[at] = jnp.zeros((BL, BL), BF)
                w_lo[at] = jnp.zeros((BL, BL), BF)

    def arrive(d, _):
        out_copy((chip + d) % CHIPS, d, chip).wait_recv()
        return 0

    lax.fori_loop(1, CHIPS, arrive, 0)

    keys_half = received.shape[0]
    base = core * keys_half

    def pair_copy(k):
        there = pl.ds(pl.multiple_of(base + k * 256, 256), 256)
        return pltpu.make_async_remote_copy(
            src_ref=keys.at[there],
            dst_ref=keys.at[there],
            send_sem=pair_send.at[k],
            recv_sem=pair_recv.at[k],
            device_id=sibling,
            device_id_type=MESH,
        )

    def whiten(k, _):
        here = pl.ds(pl.multiple_of(k * 256, 256), 256)
        there = pl.ds(pl.multiple_of(base + k * 256, 256), 256)
        parts = []
        norm = jnp.zeros((256, 1), F32)
        for j in range(4):
            deep = 256 * (j + 1)
            a = received[here, :deep]
            out = slice(256 * j, deep)
            p = dot(a, w_hi[out, :deep], 1, 1) + dot(a, w_lo[out, :deep], 1, 1) - shift[:, out]
            parts.append(p)
            norm = norm + jnp.sum(p * p, axis=1, keepdims=True)
        scale = lax.rsqrt(norm + 1e-06)
        for j in range(4):
            keys[there, 256 * j : 256 * j + 256] = (parts[j] * scale).astype(BF)
        keys[there, width:] = received[here, width:]
        pair_copy(k).start()
        return 0

    chunks = keys_half // 256
    lax.fori_loop(0, chunks, whiten, 0)

    def weights(shape, dim):
        i = lax.broadcasted_iota(jnp.int32, shape, dim)
        w = jnp.where(i == 0, 65536.0, jnp.where(i == 1, 256.0, jnp.where(i == 2, 1.0, 0.0)))
        return w.astype(BF)

    def rank_rows(first):
        here = pl.ds(pl.multiple_of(first, keys_half), keys_half)
        key_rank[:, here] = dot(weights((8, DIGITS), 1), keys[here, width:], 1, 1)

    def pair_wait(k, _):
        pair_copy(k).wait_recv()
        return 0

    rank_rows(base)
    lax.fori_loop(0, chunks, pair_wait, 0)
    rank_rows(keys_half - base)

    def score(k, _):
        here = pl.ds(pl.multiple_of(base + k * 256, 256), 256)
        q = keys[here, :width]
        q_rank = dot(keys[here, width:], weights((DIGITS, BL), 0), 1, 0)

        def part(m, best):
            there = pl.ds(pl.multiple_of(m * 512, 512), 512)
            s = dot(q, keys[there, :width], 1, 1)
            rank = key_rank[0:1, there]
            for n in range(4):
                at = slice(n * BL, (n + 1) * BL)
                best = jnp.maximum(best, jnp.where(rank[:, at] > q_rank, s[:, at], -1.0))
            return best

        best = lax.fori_loop(0, 2 * keys_half // 512, part, jnp.full((256, BL), -1.0, F32))
        top = jnp.broadcast_to(jnp.max(best, axis=1, keepdims=True), (256, BL))
        for h in range(2):
            line = jnp.sum(
                jnp.where(lane == sub, top[h * BL : (h + 1) * BL], 0.0), axis=0, keepdims=True
            )
            ret_out[2 * k + h] = bcast(line)
        return 0

    lax.fori_loop(0, chunks, score, 0)

    def ret_copy(to, at):
        return pltpu.make_async_remote_copy(
            src_ref=ret_out.at[to // 4],
            dst_ref=ret_in.at[chip],
            send_sem=ret_send.at[at],
            recv_sem=ret_recv.at[at],
            device_id=chip_device(to),
            device_id_type=MESH,
        )

    def send_back(d, _):
        ret_copy((chip + d) % CHIPS, d).start()
        return 0

    lax.fori_loop(1, CHIPS, send_back, 0)
    ret_in[chip] = ret_out[chip // 4]

    def come_back(d, _):
        ret_copy((chip + d) % CHIPS, d).wait_recv()
        return 0

    lax.fori_loop(1, CHIPS, come_back, 0)
    table = ret_in[:, 0, :]
    picks = member.astype(F32).astype(BF)
    hi = table.astype(BF)
    rest = table - hi.astype(F32)
    mid = rest.astype(BF)
    low = (rest - mid.astype(F32)).astype(BF)
    mine_of = dot(hi, picks, 0, 0) + (dot(mid, picks, 0, 0) + dot(low, picks, 0, 0))
    at_lane = lax.broadcasted_iota(jnp.int32, (BL, rows), 0) == slot + SEND * (chip % 4)
    out_ref[...] = jnp.sum(jnp.where(at_lane, mine_of, 0.0), axis=0, keepdims=True)

    swap.wait_send()
    for stage in (stage1, stage2, stage3, stage4, stage5):
        for c in stage.values():
            c.wait_send()
    for c in up:
        c.wait_send()

    def left(d, _):
        out_copy((chip + d) % CHIPS, d, chip).wait_send()
        ret_copy((chip + d) % CHIPS, d).wait_send()
        return 0

    lax.fori_loop(1, CHIPS, left, 0)

    def pair_left(k, _):
        pair_copy(k).wait_send()
        return 0

    lax.fori_loop(0, chunks, pair_left, 0)


def per_device(embeddings, clusters, doc_order):
    rows, width = embeddings.shape
    doc_count = rows * lax.axis_size("dp") * lax.axis_size("help")
    slots = CHIPS * SEND
    wide = width + DIGITS
    dma = pltpu.SemaphoreType.DMA
    vmem = pltpu.VMEM
    out = pl.pallas_call(
        lambda *refs: kernel(doc_count, *refs),
        out_shape=jax.ShapeDtypeStruct((1, rows), F32),
        in_specs=[
            pl.BlockSpec(memory_space=pl.ANY),
            pl.BlockSpec(memory_space=pltpu.VMEM),
            pl.BlockSpec(memory_space=pltpu.VMEM),
        ],
        out_specs=pl.BlockSpec(memory_space=pltpu.VMEM),
        scratch_shapes=[
            vmem((rows, width), BF),
            vmem((slots, wide), BF),
            vmem((slots, wide), BF),
            vmem((2 * slots, wide), BF),
            vmem((512, 1152), F32),
            vmem((256, 1152), F32),
            vmem((256, 1152), F32),
            vmem((3, 3, 64, 384), F32),
            vmem((3, 64, 384), F32),
            vmem((3, 3, 16, 384), F32),
            vmem((3, 4, 16, 384), F32),
            vmem((512, 1152), F32),
            vmem((width, width), F32),
            vmem((BL, BL), F32),
            vmem((width, width), BF),
            vmem((width, width), BF),
            vmem((8, 2 * slots), F32),
            vmem((16, 8, BL), F32),
            vmem((CHIPS, 8, BL), F32),
            dma,
            dma,
            dma,
            dma((45,)),
            dma((45,)),
            dma((3,)),
            dma((3,)),
            dma((CHIPS,)),
            dma((CHIPS,)),
            dma((8,)),
            dma((8,)),
            dma((CHIPS,)),
            dma((CHIPS,)),
        ],
        compiler_params=pltpu.CompilerParams(
            collective_id=0, has_side_effects=True, vmem_limit_bytes=56 * 2**20
        ),
    )(embeddings, clusters.reshape(1, rows), doc_order.reshape(1, rows))
    return out.reshape(rows)


def solution(mesh):
    in_specs = (P(("dp", "help"), None), P(("dp", "help")), P(("dp", "help")))
    out_specs = P(("dp", "help"))
    return jax.shard_map(
        per_device, mesh=mesh, in_specs=in_specs, out_specs=out_specs, check_vma=False
    )
```

```python
import jax
import jax.numpy as jnp
from jax import lax
from jax.experimental import pallas as pl
from jax.experimental.pallas import tpu as pltpu
from jax.sharding import PartitionSpec as P

F32 = jnp.float32
BF = jnp.bfloat16
MESH = pl.DeviceIdType.MESH
BL = 128
SEND = 32
CHIPS = 64
DIGITS = 128
AXES = ("x", "y", "z")
PLACE = (8, 0, 0, 0, 0, 0)
EARLY = (0, 0, 0, 0, 0)
FEED_STEP = 16
FEED_STEPS = 8


def dot(a, b, ca, cb):
    return lax.dot_general(a, b, (((ca,), (cb,)), ((), ())), preferred_element_type=F32)


def dot_full(a, b, ca, cb):
    return lax.dot_general(
        a,
        b,
        (((ca,), (cb,)), ((), ())),
        precision=lax.Precision.HIGHEST,
        preferred_element_type=F32,
    )


def bcast(v):
    return jnp.broadcast_to(v, (8, BL))


def sum_tree(x):
    while len(x) > 1:
        x = [x[i] + x[i + 1] for i in range(0, len(x), 2)]
    return x[0]


def split3(v):
    hi = v.astype(BF)
    rest = v - hi.astype(F32)
    mid = rest.astype(BF)
    return hi, mid, (rest - mid.astype(F32)).astype(BF)


LEFT = (0, 0, 1, 0, 2, 1)
RIGHT = (0, 1, 0, 2, 0, 1)


def stack(parts, order, axis):
    return jnp.concatenate([parts[n] for n in order], axis=axis)


GROUP = 8


def lanes(v, first):
    return [bcast(v[:, first + k : first + k + 1]) for k in range(8)]


def combine(m, v):
    return sum_tree([m[k] * bcast(v[k : k + 1]) for k in range(8)])


def chol_inverse_block(rows, between):
    sub = lax.broadcasted_iota(jnp.int32, (8, BL), 0)
    lane = lax.broadcasted_iota(jnp.int32, (8, BL), 1)
    rows = list(rows)
    out = []
    for g in range(16 // GROUP):
        norm = []
        end = GROUP * (g + 1)
        cols = lanes(rows[GROUP * g], 8 * GROUP * g)
        for p in range(GROUP * g, end):
            inside = (lane >= 8 * p) & (lane < 8 * p + 8)
            r = jnp.where(inside, jnp.where(lane == sub + 8 * p, 1.0, 0.0), rows[p])
            tf = r
            scale = jnp.zeros((8, BL), F32)
            later = lanes(rows[p], 8 * p + 8) if p + 1 < end else []
            invs = []
            for j in range(8):
                d = bcast(cols[j][j : j + 1])
                inv = 1.0 / d
                invs.append(inv)
                scale = jnp.where(sub == j, d, scale)
                times = jnp.where(sub == j, 0.0, cols[j]) * inv
                tf = tf - jnp.where(sub > j, times, 0.0) * bcast(tf[j : j + 1])
                for k in range(j + 1, 8):
                    cols[k] = cols[k] - times * bcast(cols[k][j : j + 1])
                r = r - times * bcast(r[j : j + 1])
                later = [v - times * bcast(v[j : j + 1]) for v in later]
            norm.append(tf * lax.rsqrt(scale))
            for i in range(p + 1, end):
                m = [v * invs[k] for k, v in enumerate(lanes(rows[i], 8 * p))]
                if i == p + 1:
                    pivots = lanes(rows[i], 8 * i)
                    cols = [pivots[k] - combine(m, later[k]) for k in range(8)]
                rows[i] = jnp.where(inside, 0.0, rows[i]) - combine(m, r)
            out.append(jnp.where(lane < 8 * p + 8, norm[-1], 0.0))
            between(p)
        if end < 16:
            for q in range(GROUP):
                p = GROUP * g + q
                norm[q] = jnp.where((lane >= 8 * p + 8) & (lane < 8 * end), 0.0, norm[q])
            parts = split3(jnp.concatenate(norm, axis=0))
            gone = dot(stack(parts, LEFT, 0), stack(parts, RIGHT, 0), 0, 0)
            mine = (lane >= 8 * GROUP * g) & (lane < 8 * end)
            for i in range(end, 16):
                rows[i] = jnp.where(mine, 0.0, rows[i]) - gone[8 * i : 8 * i + 8, :]
    return jnp.concatenate(out, axis=0)


def factor(m_ref, left_ref, right_ref, feed, terms=6):
    n = m_ref.shape[0]
    blocks = n // BL
    left_order, right_order = LEFT[:terms], RIGHT[:terms]

    def cut(i):
        return slice(i * BL, (i + 1) * BL)

    def deferred(p, w_stack):
        def rest_of_row(c0, c1):
            def go():
                parts = split3(m_ref[cut(p), c0:c1])
                r = dot(w_stack, stack(parts, right_order, 0), 1, 0)
                m_ref[cut(p), c0:c1] = r
                parts = split3(r)
                left_ref[:, c0:c1] = stack(parts, left_order, 0)
                right_ref[:, c0:c1] = stack(parts, right_order, 0)
            return go
        def trail(i):
            def go():
                lhs = left_ref[:, cut(i)]
                m_ref[cut(i), cut(p)] = jnp.zeros((BL, BL), F32)
                low = slice(0, (p + 1) * BL)
                m_ref[cut(i), low] = m_ref[cut(i), low] - dot(lhs, right_ref[:, low], 0, 0)
                first = i + 1 if i == p + 1 else i
                if first < blocks:
                    up = slice(first * BL, n)
                    m_ref[cut(i), up] = m_ref[cut(i), up] - dot(lhs, right_ref[:, up], 0, 0)
            return go
        todo = []
        if p > 0:
            todo.append(rest_of_row(0, p * BL))
        if p + 2 < blocks:
            todo.append(rest_of_row((p + 2) * BL, n))
        return todo + [trail(i) for i in range(p + 1, blocks)]

    todo = []
    for p in range(blocks):
        feed(p)
        count = len(todo)
        done = [0]

        def between(q):
            upto = -(-count * (q + 1) // 13)
            while done[0] < min(upto, count):
                todo[done[0]]()
                done[0] += 1

        w = chol_inverse_block([m_ref[p * BL + 8 * i : p * BL + 8 * i + 8, cut(p)] for i in range(16)], between)
        w_parts = split3(w)
        w_stack = stack(w_parts, left_order, 1)
        if p + 1 < blocks:
            nxt = cut(p + 1)
            parts = split3(m_ref[cut(p), nxt])
            r = dot(w_stack, stack(parts, right_order, 0), 1, 0)
            m_ref[cut(p), nxt] = r
            parts = split3(r)
            lhs, rhs = stack(parts, left_order, 0), stack(parts, right_order, 0)
            left_ref[:, nxt] = lhs
            right_ref[:, nxt] = rhs
            m_ref[nxt, nxt] = m_ref[nxt, nxt] - dot(lhs, rhs, 0, 0)
            left_ref[:, cut(p)] = stack(w_parts, left_order, 0)
            right_ref[:, cut(p)] = stack(w_parts, right_order, 0)
        elif p > 0:
            parts = split3(m_ref[cut(p), : p * BL])
            m_ref[cut(p), : p * BL] = dot(w_stack, stack(parts, right_order, 0), 1, 0)
        m_ref[cut(p), cut(p)] = w
        todo = deferred(p, w_stack)


def place(i):
    return min(i, 7 - i) * BL, 0 if i < 4 else (i + 1) * BL


def slots_of(clusters_row):
    n = clusters_row.shape[1]
    member = lax.broadcasted_iota(jnp.int32, (CHIPS, n), 0) == clusters_row
    before = lax.broadcasted_iota(jnp.int32, (n, n), 0) < lax.broadcasted_iota(jnp.int32, (n, n), 1)
    count = dot(member.astype(F32).astype(BF), before.astype(F32).astype(BF), 1, 0)
    slot = jnp.sum(jnp.where(member, count, 0.0), axis=0, keepdims=True)
    return member, slot.astype(jnp.int32)


def digits_of(order_row, doc_count):
    n = order_row.shape[1]
    value = doc_count - order_row
    row = lax.broadcasted_iota(jnp.int32, (DIGITS, n), 0)
    d = jnp.where(row == 0, value >> 16, jnp.where(row == 1, (value >> 8) & 255, value & 255))
    return jnp.where(row < 3, d, 0).astype(F32).T.astype(BF)


def kernel(
    doc_count,
    emb_ref,
    clusters_ref,
    order_ref,
    out_ref,
    emb,
    outgoing,
    received,
    keys,
    packed,
    half_in,
    acc,
    in1,
    sum1,
    in2,
    in3,
    total,
    mat,
    left_ref,
    right_ref,
    w_hi,
    w_lo,
    key_rank,
    row_best,
    col_best,
    cross_col,
    cross_out,
    cross_in,
    ret_out,
    ret_in,
    emb_sem,
    core_send,
    core_recv,
    ring_send,
    ring_recv,
    up_send,
    up_recv,
    out_send,
    out_recv,
    pair_send,
    pair_recv,
    share_send,
    share_recv,
    ret_send,
    ret_recv,
):
    dp = lax.axis_index("dp")
    y = lax.axis_index("help")
    core = dp % 2
    x = dp // 8
    z = (dp // 2) % 4
    chip = (dp // 2) * 4 + y
    sibling = (dp + 1 - 2 * core, y)
    rows = emb.shape[0]
    width = emb.shape[1]

    def chip_device(c):
        return ((c // 4) * 2 + core, c % 4)

    def partner(d):
        d = (d * 27) % CHIPS
        return ((x + d // 16) % 4 * 4 + (z + d // 4) % 4) * 4 + (y + d) % 4

    def axis_peer(axis, d):
        if axis == "x":
            to = (x + d) % 4
            return ((to * 4 + z) * 2 + core, y), to
        if axis == "z":
            to = (z + d) % 4
            return ((x * 4 + to) * 2 + core, y), to
        to = (y + d) % 4
        return (dp, to), to

    place_on = {"x": x, "y": y, "z": z}

    barrier = pltpu.get_barrier_semaphore()

    def greet(d, _):
        pl.semaphore_signal(
            barrier, inc=1, device_id=chip_device(partner(d)), device_id_type=MESH
        )
        return 0

    lax.fori_loop(1, CHIPS, greet, 0)
    pl.semaphore_signal(barrier, inc=1, device_id=sibling, device_id_type=MESH)
    load = pltpu.make_async_copy(emb_ref, emb, emb_sem)
    load.start()
    member, slot = slots_of(clusters_ref[...])
    target = clusters_ref[...] * SEND + slot
    digits = digits_of(order_ref[...], doc_count)
    load.wait()

    col_sum = dot(jnp.ones((8, rows), BF), emb[...], 1, 0)
    sub = lax.broadcasted_iota(jnp.int32, (BL, BL), 0)
    lane = lax.broadcasted_iota(jnp.int32, (BL, BL), 1)
    for b in range(width // 256):
        block = dot(emb[:, 256 * b : 256 * b + 256], emb[:, 256 * b :], 0, 0)
        for i in (2 * b, 2 * b + 1):
            r0, c0 = place(i)
            skip = (i - 2 * b) * BL
            part = block[skip : skip + BL, skip:]
            w = part.shape[1]
            packed[r0 : r0 + BL, c0 : c0 + w] = part
            cs = jnp.broadcast_to(col_sum[0:1, i * BL : i * BL + BL], (BL, BL))
            spare = jnp.where(sub == BL - 2, cs, pltpu.roll(cs, 64, 1))
            use = (sub >= BL - 2) & (lane < 64)
            packed[r0 : r0 + BL, c0 : c0 + BL] = jnp.where(use, spare, part[:, :BL])

    placed = [0]

    def place_at(n):
        first = placed[0]
        placed[0] = first + PLACE[n]
        if PLACE[n]:
            lax.fori_loop(first, placed[0], place_rows, 0)

    def place_rows(k, _):
        first = pl.multiple_of(k * 256, 256)
        here = lax.broadcasted_iota(jnp.int32, (256, rows), 0) + first
        pick = (here == target).astype(F32).astype(BF)
        outgoing[pl.ds(first, 256), 0:width] = dot(pick, emb[...], 1, 0).astype(BF)
        outgoing[pl.ds(first, 256), width:] = dot(pick, digits, 1, 0).astype(BF)
        return 0

    place_at(0)
    pl.semaphore_wait(barrier, CHIPS)

    half = packed.shape[0] // 2
    mine = pl.ds(pl.multiple_of(core * half, 8), half)
    other = pl.ds(pl.multiple_of((1 - core) * half, 8), half)
    swap = pltpu.make_async_remote_copy(
        src_ref=packed.at[other],
        dst_ref=half_in,
        send_sem=core_send,
        recv_sem=core_recv,
        device_id=sibling,
        device_id_type=MESH,
    )
    swap.start()

    place_at(1)
    swap.wait_recv()
    acc[...] = packed[mine, :] + half_in[...]

    def out_copy(to, at, source):
        return pltpu.make_async_remote_copy(
            src_ref=outgoing.at[pl.ds(pl.multiple_of(to * SEND, SEND), SEND), :],
            dst_ref=received.at[pl.ds(pl.multiple_of(source * SEND, SEND), SEND), :],
            send_sem=out_send.at[at],
            recv_sem=out_recv.at[at],
            device_id=chip_device(to),
            device_id_type=MESH,
        )

    def send_out(d, _):
        out_copy(partner(d), d, chip).start()
        return 0

    sent_out = [1]

    def feed(count):
        first = sent_out[0]
        sent_out[0] = min(first + count, CHIPS)
        if sent_out[0] > first:
            lax.fori_loop(first, sent_out[0], send_out, 0)

    def ring_copy(stage, q, d, src, dst, device):
        return pltpu.make_async_remote_copy(
            src_ref=src,
            dst_ref=dst,
            send_sem=ring_send.at[stage * 9 + q * 3 + d - 1],
            recv_sem=ring_recv.at[stage * 9 + q * 3 + d - 1],
            device_id=device,
            device_id_type=MESH,
        )

    third = acc.shape[1] // 3
    cols = [slice(q * third, (q + 1) * third) for q in range(3)]
    axis_a = [AXES[q] for q in range(3)]
    axis_b = [AXES[(q + 1) % 3] for q in range(3)]
    axis_c = [AXES[(q + 2) % 3] for q in range(3)]
    sent = []
    stage1 = {}
    for d in (2, 1, 3):
        for q in range(3):
            device, to = axis_peer(axis_a[q], d)
            src = acc.at[pl.ds(pl.multiple_of(to * 64, 64), 64), cols[q]]
            c = ring_copy(0, q, d, src, in1.at[q, d - 1], device)
            c.start()
            stage1[q, d] = c
    place_at(2)
    feed(EARLY[1])
    stage2 = {}
    for q in range(3):
        for d in (1, 3, 2):
            stage1[q, d].wait_recv()
        a = place_on[axis_a[q]]
        own = acc[pl.ds(pl.multiple_of(a * 64, 64), 64), cols[q]]
        sum1[q] = (own + in1[q, 0]) + (in1[q, 1] + in1[q, 2])
        for d in (2, 1, 3):
            device, to = axis_peer(axis_b[q], d)
            src = sum1.at[q, pl.ds(pl.multiple_of(to * 16, 16), 16), :]
            c = ring_copy(1, q, d, src, in2.at[q, d - 1], device)
            c.start()
            stage2[q, d] = c
    place_at(3)
    feed(EARLY[2])
    stage3 = {}
    for q in range(3):
        for d in (1, 3, 2):
            stage2[q, d].wait_recv()
        b = place_on[axis_b[q]]
        c_at = place_on[axis_c[q]]
        own = sum1[q, pl.ds(pl.multiple_of(b * 16, 16), 16), :]
        in3[q, c_at] = (own + in2[q, 0]) + (in2[q, 1] + in2[q, 2])
        for d in (2, 1, 3):
            device, to = axis_peer(axis_c[q], d)
            c = ring_copy(2, q, d, in3.at[q, c_at], in3.at[q, c_at], device)
            c.start()
            stage3[q, d] = c
    place_at(4)
    feed(EARLY[3])
    stage4 = {}
    for q in range(3):
        for d in (1, 3, 2):
            stage3[q, d].wait_recv()
        a, b = place_on[axis_a[q]], place_on[axis_b[q]]
        there = pl.ds(pl.multiple_of(core * half + a * 64 + b * 16, 16), 16)
        total[there, cols[q]] = (in3[q, 0] + in3[q, 1]) + (in3[q, 2] + in3[q, 3])
        for d in (2, 1, 3):
            device, to = axis_peer(axis_b[q], d)
            c = ring_copy(3, q, d, total.at[there, cols[q]], total.at[there, cols[q]], device)
            c.start()
            stage4[q, d] = c
    place_at(5)
    feed(EARLY[4])
    stage5 = {}
    for q in range(3):
        for d in (1, 3, 2):
            stage4[q, d].wait_recv()
        a = place_on[axis_a[q]]
        there = pl.ds(pl.multiple_of(core * half + a * 64, 64), 64)
        for d in (2, 1, 3):
            device, to = axis_peer(axis_a[q], d)
            c = ring_copy(4, q, d, total.at[there, cols[q]], total.at[there, cols[q]], device)
            c.start()
            stage5[q, d] = c
    up = []
    for q in range(3):
        for d in (1, 3, 2):
            stage5[q, d].wait_recv()
        c = pltpu.make_async_remote_copy(
            src_ref=total.at[mine, cols[q]],
            dst_ref=total.at[mine, cols[q]],
            send_sem=up_send.at[q],
            recv_sem=up_recv.at[q],
            device_id=sibling,
            device_id_type=MESH,
        )
        c.start()
        up.append(c)

    own_rows = pl.ds(pl.multiple_of(chip * SEND, SEND), SEND)
    received[own_rows, :] = outgoing[own_rows, :]
    for c in up:
        c.wait_recv()

    inv_n = 1.0 / doc_count
    center = []
    trace = jnp.zeros((BL, BL), F32)
    for i in range(8):
        r0, c0 = place(i)
        d = total[r0 : r0 + BL, c0 : c0 + BL]
        tail = d[BL - 8 :, :]
        c = jnp.where(lane[:1] < 64, tail[6:7], pltpu.roll(tail, 64, 1)[7:8]) * inv_n
        center.append(c)
        cb = jnp.broadcast_to(c, (BL, BL))
        trace = trace + jnp.where(lane == sub, d * inv_n - cb * cb, 0.0)
    trace = jnp.sum(jnp.sum(trace, axis=1, keepdims=True), axis=0, keepdims=True)
    ridge = 0.001 * trace * (1.0 / width)
    for i in range(8):
        r0, c0 = place(i)
        col = jnp.broadcast_to(center[i], (BL, BL)).T
        for j in range(i, 8):
            g = total[r0 : r0 + BL, c0 + (j - i) * BL : c0 + (j - i + 1) * BL]
            if j == i:
                g = jnp.where(lane >= sub, g, g.T)
            v = g * inv_n - col * center[j]
            if j == i:
                v = v + jnp.where(lane == sub, ridge, 0.0)
            mat[i * BL : (i + 1) * BL, j * BL : (j + 1) * BL] = v
        for j in range(i):
            mat[i * BL : (i + 1) * BL, j * BL : (j + 1) * BL] = jnp.zeros((BL, BL), F32)
    factor(mat, left_ref, right_ref, lambda p: feed(FEED_STEP) if p < FEED_STEPS else None)
    feed(CHIPS)
    shift = []
    for j in range(8):
        shift.append(
            dot_full(
                jnp.concatenate([jnp.broadcast_to(c, (8, BL)) for c in center[: j + 1]], axis=1),
                mat[j * BL : (j + 1) * BL, : (j + 1) * BL],
                1,
                1,
            )[0:1]
        )
    shift = jnp.concatenate(shift, axis=1)
    for i in range(8):
        for j in range(8):
            at = (slice(i * BL, (i + 1) * BL), slice(j * BL, (j + 1) * BL))
            if j <= i:
                v = mat[at]
                hi = v.astype(BF)
                w_hi[at] = hi
                w_lo[at] = (v - hi.astype(F32)).astype(BF)
            else:
                w_hi[at] = jnp.zeros((BL, BL), BF)
                w_lo[at] = jnp.zeros((BL, BL), BF)

    def arrive(d, _):
        out_copy(partner(d), d, chip).wait_recv()
        return 0

    lax.fori_loop(1, CHIPS, arrive, 0)

    keys_half = received.shape[0]
    base = core * keys_half

    def pair_copy(k):
        there = pl.ds(pl.multiple_of(base + k * 1024, 1024), 1024)
        return pltpu.make_async_remote_copy(
            src_ref=keys.at[there],
            dst_ref=keys.at[there],
            send_sem=pair_send.at[k],
            recv_sem=pair_recv.at[k],
            device_id=sibling,
            device_id_type=MESH,
        )

    def whiten(k, _):
        here = pl.ds(pl.multiple_of(k * 1024, 1024), 1024)
        there = pl.ds(pl.multiple_of(base + k * 1024, 1024), 1024)
        parts = []
        norm = jnp.zeros((1024, 1), F32)
        for j in range(4):
            deep = 256 * (j + 1)
            a = received[here, :deep]
            out = slice(256 * j, deep)
            p = dot(a, w_hi[out, :deep], 1, 1) + dot(a, w_lo[out, :deep], 1, 1) - shift[:, out]
            parts.append(p)
            norm = norm + jnp.sum(p * p, axis=1, keepdims=True)
        scale = lax.rsqrt(norm + 1e-06)
        for j in range(4):
            keys[there, 256 * j : 256 * j + 256] = (parts[j] * scale).astype(BF)
        keys[there, width:] = received[here, width:]
        pair_copy(k).start()
        return 0

    chunks = keys_half // 1024
    lax.fori_loop(0, chunks, whiten, 0)

    def weights(shape, dim):
        i = lax.broadcasted_iota(jnp.int32, shape, dim)
        w = jnp.where(i == 0, 65536.0, jnp.where(i == 1, 256.0, jnp.where(i == 2, 1.0, 0.0)))
        return w.astype(BF)

    def rank_rows(first):
        here = pl.ds(pl.multiple_of(first, keys_half), keys_half)
        key_rank[:, here] = dot(weights((8, DIGITS), 1), keys[here, width:], 1, 1)

    def pair_wait(k, _):
        pair_copy(k).wait_recv()
        return 0

    rank_rows(base)
    row_best[...] = jnp.full(row_best.shape, -1.0, F32)
    col_best[...] = jnp.full(col_best.shape, -1.0, F32)

    def rank_columns(rows_at):
        return dot(keys[rows_at, width:], weights((DIGITS, BL), 0), 1, 0)

    def tile(q_rank, scores, rank, row, diagonal):
        n = scores.shape[0]
        cols = []
        for c in range(scores.shape[1] // BL):
            at = slice(c * BL, (c + 1) * BL)
            earlier = rank[:, at] > q_rank
            row = jnp.maximum(row, jnp.where(earlier, scores[:, at], -1.0))
            if c * BL >= diagonal:
                back = jnp.where(earlier, -1.0, scores[:, at])
                cols.append(jnp.max(back.reshape(n // 8, 8, BL), axis=0))
        return row, cols

    for a in range(4):
        q_at = pl.ds(pl.multiple_of(base + 512 * a, 512), 512)
        left = 512 * a
        k_at = pl.ds(pl.multiple_of(base + left, 512), keys_half - left)
        scores = dot(keys[q_at, :width], keys[k_at, :width], 1, 1)
        row, cols = tile(rank_columns(q_at), scores, key_rank[0:1, k_at], row_best[512 * a : 512 * a + 512, :], 512)
        row_best[512 * a : 512 * a + 512, :] = row
        for c, v in enumerate(cols):
            at = slice(left + 512 + c * BL, left + 512 + (c + 1) * BL)
            col_best[:, at] = jnp.maximum(col_best[:, at], v)
    lax.fori_loop(0, chunks, pair_wait, 0)
    rank_rows(keys_half - base)

    cross_at = pl.ds(pl.multiple_of(core * 1024, 1024), 1024)

    def cross(t, _):
        k_at = pl.ds(pl.multiple_of(keys_half + 512 * t, 512), 512)
        c_at = pl.ds(pl.multiple_of(512 * t, 512), 512)
        scores = dot(keys[cross_at, :width], keys[k_at, :width], 1, 1)
        here = slice(keys_half, keys_half + 1024)
        row, cols = tile(rank_columns(cross_at), scores, key_rank[0:1, k_at], row_best[here, :], 0)
        row_best[here, :] = row
        cross_col[:, c_at] = jnp.concatenate(cols, axis=1)
        return 0

    lax.fori_loop(0, keys_half // 512, cross, 0)

    def line_of(g):
        top = row_best[g * BL : (g + 1) * BL, :]
        top = jnp.broadcast_to(jnp.max(top, axis=1, keepdims=True), (BL, BL))
        return jnp.sum(jnp.where(lane == sub, top, 0.0), axis=0, keepdims=True)

    for g in range(8):
        cross_out[g : g + 1, :] = line_of(16 + g)
    for g in range(16):
        at = slice(g * BL, (g + 1) * BL)
        cross_out[8 + g : 9 + g, :] = jnp.max(cross_col[:, at], axis=0, keepdims=True)
    share = pltpu.make_async_remote_copy(
        src_ref=cross_out,
        dst_ref=cross_in,
        send_sem=share_send,
        recv_sem=share_recv,
        device_id=sibling,
        device_id_type=MESH,
    )
    share.start()
    lines = []
    for g in range(16):
        at = slice(g * BL, (g + 1) * BL)
        lines.append(jnp.maximum(line_of(g), jnp.max(col_best[:, at], axis=0, keepdims=True)))
    lines = jnp.concatenate(lines, axis=0)
    share.wait_recv()
    first = jnp.concatenate([cross_out[0:8, :], cross_in[0:8, :]], axis=0)
    second = jnp.maximum(cross_out[8:24, :], cross_in[8:24, :])
    lines = jnp.maximum(lines, jnp.where(core == 0, first, second))
    for g in range(16):
        ret_out[g] = bcast(lines[g : g + 1, :])

    def ret_copy(to, at):
        return pltpu.make_async_remote_copy(
            src_ref=ret_out.at[to // 4],
            dst_ref=ret_in.at[chip],
            send_sem=ret_send.at[at],
            recv_sem=ret_recv.at[at],
            device_id=chip_device(to),
            device_id_type=MESH,
        )

    def send_back(d, _):
        ret_copy(partner(d), d).start()
        return 0

    lax.fori_loop(1, CHIPS, send_back, 0)
    ret_in[chip] = ret_out[chip // 4]

    def come_back(d, _):
        ret_copy(partner(d), d).wait_recv()
        return 0

    lax.fori_loop(1, CHIPS, come_back, 0)
    table = ret_in[:, 0, :]
    picks = member.astype(F32).astype(BF)
    hi = table.astype(BF)
    rest = table - hi.astype(F32)
    mid = rest.astype(BF)
    low = (rest - mid.astype(F32)).astype(BF)
    mine_of = dot(hi, picks, 0, 0) + (dot(mid, picks, 0, 0) + dot(low, picks, 0, 0))
    at_lane = lax.broadcasted_iota(jnp.int32, (BL, rows), 0) == slot + SEND * (chip % 4)
    out_ref[...] = jnp.sum(jnp.where(at_lane, mine_of, 0.0), axis=0, keepdims=True)

    swap.wait_send()
    share.wait_send()
    for stage in (stage1, stage2, stage3, stage4, stage5):
        for c in stage.values():
            c.wait_send()
    for c in up:
        c.wait_send()

    def left(d, _):
        out_copy(partner(d), d, chip).wait_send()
        ret_copy(partner(d), d).wait_send()
        return 0

    lax.fori_loop(1, CHIPS, left, 0)

    def pair_left(k, _):
        pair_copy(k).wait_send()
        return 0

    lax.fori_loop(0, chunks, pair_left, 0)


def per_device(embeddings, clusters, doc_order):
    rows, width = embeddings.shape
    doc_count = rows * lax.axis_size("dp") * lax.axis_size("help")
    slots = CHIPS * SEND
    wide = width + DIGITS
    dma = pltpu.SemaphoreType.DMA
    vmem = pltpu.VMEM
    out = pl.pallas_call(
        lambda *refs: kernel(doc_count, *refs),
        out_shape=jax.ShapeDtypeStruct((1, rows), F32),
        in_specs=[
            pl.BlockSpec(memory_space=pl.ANY),
            pl.BlockSpec(memory_space=pltpu.VMEM),
            pl.BlockSpec(memory_space=pltpu.VMEM),
        ],
        out_specs=pl.BlockSpec(memory_space=pltpu.VMEM),
        scratch_shapes=[
            vmem((rows, width), BF),
            vmem((slots, wide), BF),
            vmem((slots, wide), BF),
            vmem((2 * slots, wide), BF),
            vmem((512, 1152), F32),
            vmem((256, 1152), F32),
            vmem((256, 1152), F32),
            vmem((3, 3, 64, 384), F32),
            vmem((3, 64, 384), F32),
            vmem((3, 3, 16, 384), F32),
            vmem((3, 4, 16, 384), F32),
            vmem((512, 1152), F32),
            vmem((width, width), F32),
            vmem((6 * BL, width), BF),
            vmem((6 * BL, width), BF),
            vmem((width, width), BF),
            vmem((width, width), BF),
            vmem((8, 2 * slots), F32),
            vmem((slots + 1024, BL), F32),
            vmem((8, slots), F32),
            vmem((8, slots), F32),
            vmem((24, BL), F32),
            vmem((24, BL), F32),
            vmem((16, 8, BL), F32),
            vmem((CHIPS, 8, BL), F32),
            dma,
            dma,
            dma,
            dma((45,)),
            dma((45,)),
            dma((3,)),
            dma((3,)),
            dma((CHIPS,)),
            dma((CHIPS,)),
            dma((2,)),
            dma((2,)),
            dma,
            dma,
            dma((CHIPS,)),
            dma((CHIPS,)),
        ],
        compiler_params=pltpu.CompilerParams(
            collective_id=0, has_side_effects=True, vmem_limit_bytes=56 * 2**20
        ),
    )(embeddings, clusters.reshape(1, rows), doc_order.reshape(1, rows))
    return out.reshape(rows)


def solution(mesh):
    in_specs = (P(("dp", "help"), None), P(("dp", "help")), P(("dp", "help")))
    out_specs = P(("dp", "help"))
    return jax.shard_map(
        per_device, mesh=mesh, in_specs=in_specs, out_specs=out_specs, check_vma=False
    )
```

```python
import jax
import jax.numpy as jnp
from jax import lax
from jax.experimental import pallas as pl
from jax.experimental.pallas import tpu as pltpu
from jax.sharding import PartitionSpec as P

F32 = jnp.float32
BF = jnp.bfloat16
MESH = pl.DeviceIdType.MESH
BL = 128
SEND = 32
CHIPS = 64
DIGITS = 128
AXES = ("x", "y", "z")
PLACE = (0, 2, 3, 1, 1, 1)
EARLY = (0, 0, 0, 0, 0)
FEED_STEP = 16
MIX, UNMIX = 27, 19
CHUNK = 512
FEED_STEPS = 8


def dot(a, b, ca, cb):
    return lax.dot_general(a, b, (((ca,), (cb,)), ((), ())), preferred_element_type=F32)


def dot_full(a, b, ca, cb):
    return lax.dot_general(
        a,
        b,
        (((ca,), (cb,)), ((), ())),
        precision=lax.Precision.HIGHEST,
        preferred_element_type=F32,
    )


def bcast(v):
    return jnp.broadcast_to(v, (8, BL))


def sum_tree(x):
    while len(x) > 1:
        x = [x[i] + x[i + 1] for i in range(0, len(x), 2)]
    return x[0]


def split3(v):
    hi = v.astype(BF)
    rest = v - hi.astype(F32)
    mid = rest.astype(BF)
    return hi, mid, (rest - mid.astype(F32)).astype(BF)


LEFT = (0, 0, 1, 0, 2, 1)
RIGHT = (0, 1, 0, 2, 0, 1)


def stack(parts, order, axis):
    return jnp.concatenate([parts[n] for n in order], axis=axis)


GROUP = 8


def lanes(v, first):
    return [bcast(v[:, first + k : first + k + 1]) for k in range(8)]


def combine(m, v):
    return sum_tree([m[k] * bcast(v[k : k + 1]) for k in range(8)])


def chol_inverse_block(rows, between):
    sub = lax.broadcasted_iota(jnp.int32, (8, BL), 0)
    lane = lax.broadcasted_iota(jnp.int32, (8, BL), 1)
    rows = list(rows)
    out = []
    for g in range(16 // GROUP):
        norm = []
        end = GROUP * (g + 1)
        cols = lanes(rows[GROUP * g], 8 * GROUP * g)
        for p in range(GROUP * g, end):
            inside = (lane >= 8 * p) & (lane < 8 * p + 8)
            r = jnp.where(inside, jnp.where(lane == sub + 8 * p, 1.0, 0.0), rows[p])
            tf = r
            scale = jnp.zeros((8, BL), F32)
            later = lanes(rows[p], 8 * p + 8) if p + 1 < end else []
            invs = []
            for j in range(8):
                d = bcast(cols[j][j : j + 1])
                inv = 1.0 / d
                invs.append(inv)
                scale = jnp.where(sub == j, d, scale)
                times = jnp.where(sub == j, 0.0, cols[j]) * inv
                tf = tf - jnp.where(sub > j, times, 0.0) * bcast(tf[j : j + 1])
                for k in range(j + 1, 8):
                    cols[k] = cols[k] - times * bcast(cols[k][j : j + 1])
                r = r - times * bcast(r[j : j + 1])
                later = [v - times * bcast(v[j : j + 1]) for v in later]
            norm.append(tf * lax.rsqrt(scale))
            for i in range(p + 1, end):
                m = [v * invs[k] for k, v in enumerate(lanes(rows[i], 8 * p))]
                if i == p + 1:
                    pivots = lanes(rows[i], 8 * i)
                    cols = [pivots[k] - combine(m, later[k]) for k in range(8)]
                rows[i] = jnp.where(inside, 0.0, rows[i]) - combine(m, r)
            out.append(jnp.where(lane < 8 * p + 8, norm[-1], 0.0))
            between(p)
        if end < 16:
            for q in range(GROUP):
                p = GROUP * g + q
                norm[q] = jnp.where((lane >= 8 * p + 8) & (lane < 8 * end), 0.0, norm[q])
            parts = split3(jnp.concatenate(norm, axis=0))
            gone = dot(stack(parts, LEFT, 0), stack(parts, RIGHT, 0), 0, 0)
            mine = (lane >= 8 * GROUP * g) & (lane < 8 * end)
            for i in range(end, 16):
                rows[i] = jnp.where(mine, 0.0, rows[i]) - gone[8 * i : 8 * i + 8, :]
    return jnp.concatenate(out, axis=0)


def factor(m_ref, left_ref, right_ref, feed, terms=6):
    n = m_ref.shape[0]
    blocks = n // BL
    left_order, right_order = LEFT[:terms], RIGHT[:terms]

    def cut(i):
        return slice(i * BL, (i + 1) * BL)

    def deferred(p, w_stack):
        def rest_of_row(c0, c1):
            def go():
                parts = split3(m_ref[cut(p), c0:c1])
                r = dot(w_stack, stack(parts, right_order, 0), 1, 0)
                m_ref[cut(p), c0:c1] = r
                parts = split3(r)
                left_ref[:, c0:c1] = stack(parts, left_order, 0)
                right_ref[:, c0:c1] = stack(parts, right_order, 0)
            return go
        def trail(i):
            def go():
                lhs = left_ref[:, cut(i)]
                m_ref[cut(i), cut(p)] = jnp.zeros((BL, BL), F32)
                low = slice(0, (p + 1) * BL)
                m_ref[cut(i), low] = m_ref[cut(i), low] - dot(lhs, right_ref[:, low], 0, 0)
                first = i + 1 if i == p + 1 else i
                if first < blocks:
                    up = slice(first * BL, n)
                    m_ref[cut(i), up] = m_ref[cut(i), up] - dot(lhs, right_ref[:, up], 0, 0)
            return go
        todo = []
        if p > 0:
            todo.append(rest_of_row(0, p * BL))
        if p + 2 < blocks:
            todo.append(rest_of_row((p + 2) * BL, n))
        return todo + [trail(i) for i in range(p + 1, blocks)]

    todo = []
    for p in range(blocks):
        feed(p)
        count = len(todo)
        done = [0]

        def between(q):
            upto = -(-count * (q + 1) // 13)
            while done[0] < min(upto, count):
                todo[done[0]]()
                done[0] += 1

        w = chol_inverse_block([m_ref[p * BL + 8 * i : p * BL + 8 * i + 8, cut(p)] for i in range(16)], between)
        w_parts = split3(w)
        w_stack = stack(w_parts, left_order, 1)
        if p + 1 < blocks:
            nxt = cut(p + 1)
            parts = split3(m_ref[cut(p), nxt])
            r = dot(w_stack, stack(parts, right_order, 0), 1, 0)
            m_ref[cut(p), nxt] = r
            parts = split3(r)
            lhs, rhs = stack(parts, left_order, 0), stack(parts, right_order, 0)
            left_ref[:, nxt] = lhs
            right_ref[:, nxt] = rhs
            m_ref[nxt, nxt] = m_ref[nxt, nxt] - dot(lhs, rhs, 0, 0)
            left_ref[:, cut(p)] = stack(w_parts, left_order, 0)
            right_ref[:, cut(p)] = stack(w_parts, right_order, 0)
        elif p > 0:
            parts = split3(m_ref[cut(p), : p * BL])
            m_ref[cut(p), : p * BL] = dot(w_stack, stack(parts, right_order, 0), 1, 0)
        m_ref[cut(p), cut(p)] = w
        todo = deferred(p, w_stack)


def place(i):
    return min(i, 7 - i) * BL, 0 if i < 4 else (i + 1) * BL


def slots_of(clusters_row):
    n = clusters_row.shape[1]
    member = lax.broadcasted_iota(jnp.int32, (CHIPS, n), 0) == clusters_row
    before = lax.broadcasted_iota(jnp.int32, (n, n), 0) < lax.broadcasted_iota(jnp.int32, (n, n), 1)
    count = dot(member.astype(F32).astype(BF), before.astype(F32).astype(BF), 1, 0)
    slot = jnp.sum(jnp.where(member, count, 0.0), axis=0, keepdims=True)
    return member, slot.astype(jnp.int32)


def digits_of(order_row, doc_count):
    n = order_row.shape[1]
    value = doc_count - order_row
    row = lax.broadcasted_iota(jnp.int32, (DIGITS, n), 0)
    d = jnp.where(row == 0, value >> 16, jnp.where(row == 1, (value >> 8) & 255, value & 255))
    return jnp.where(row < 3, d, 0).astype(F32).T.astype(BF)


def kernel(
    doc_count,
    emb_ref,
    clusters_ref,
    order_ref,
    out_ref,
    emb,
    outgoing,
    received,
    keys,
    packed,
    half_in,
    acc,
    in1,
    sum1,
    in2,
    in3,
    total,
    mat,
    left_ref,
    right_ref,
    w_hi,
    w_lo,
    key_rank,
    row_best,
    col_best,
    cross_row,
    cross_col,
    cross_out,
    cross_in,
    ret_out,
    ret_in,
    emb_sem,
    core_send,
    core_recv,
    ring_send,
    ring_recv,
    up_send,
    up_recv,
    out_send,
    out_recv,
    pair_send,
    pair_recv,
    share_send,
    share_recv,
    ret_send,
    ret_recv,
):
    dp = lax.axis_index("dp")
    y = lax.axis_index("help")
    core = dp % 2
    x = dp // 8
    z = (dp // 2) % 4
    chip = (dp // 2) * 4 + y
    sibling = (dp + 1 - 2 * core, y)
    rows = emb.shape[0]
    width = emb.shape[1]

    def chip_device(c):
        return ((c >> 2) * 2 + core, c & 3)

    def chip_at(dx, dy, dz):
        return (((x + dx) & 3) * 4 + ((z + dz) & 3)) * 4 + ((y + dy) & 3)

    def partner(d):
        d = d * MIX % CHIPS
        return chip_at(d // 16, d % 4, d // 4 % 4)

    def source(d):
        d = d * MIX % CHIPS
        return chip_at(4 - d // 16, 4 - d % 4, 4 - d // 4 % 4)

    def axis_peer(axis, d):
        if axis == "x":
            to = (x + d) % 4
            return ((to * 4 + z) * 2 + core, y), to
        if axis == "z":
            to = (z + d) % 4
            return ((x * 4 + to) * 2 + core, y), to
        to = (y + d) % 4
        return (dp, to), to

    place_on = {"x": x, "y": y, "z": z}

    barrier = pltpu.get_barrier_semaphore()

    for axis in AXES:
        for d in (1, 2, 3):
            device, _ = axis_peer(axis, d)
            pl.semaphore_signal(barrier, inc=1, device_id=device, device_id_type=MESH)
    pl.semaphore_signal(barrier, inc=1, device_id=sibling, device_id_type=MESH)
    load = pltpu.make_async_copy(emb_ref, emb, emb_sem)
    load.start()
    label = clusters_ref[...]
    label = (
        (label // 16 - x + 4) % 4 * 16 + (label // 4 % 4 - z + 4) % 4 * 4 + (label % 4 - y + 4) % 4
    ) * UNMIX % CHIPS
    member, slot = slots_of(label)
    target = label * SEND + slot
    digits = digits_of(order_ref[...], doc_count)
    load.wait()

    col_sum = dot(jnp.ones((8, rows), BF), emb[...], 1, 0)
    sub = lax.broadcasted_iota(jnp.int32, (BL, BL), 0)
    lane = lax.broadcasted_iota(jnp.int32, (BL, BL), 1)
    for b in range(width // 256):
        block = dot(emb[:, 256 * b : 256 * b + 256], emb[:, 256 * b :], 0, 0)
        for i in (2 * b, 2 * b + 1):
            r0, c0 = place(i)
            skip = (i - 2 * b) * BL
            part = block[skip : skip + BL, skip:]
            w = part.shape[1]
            packed[r0 : r0 + BL, c0 : c0 + w] = part
            cs = jnp.broadcast_to(col_sum[0:1, i * BL : i * BL + BL], (BL, BL))
            spare = jnp.where(sub == BL - 2, cs, pltpu.roll(cs, 64, 1))
            use = (sub >= BL - 2) & (lane < 64)
            packed[r0 : r0 + BL, c0 : c0 + BL] = jnp.where(use, spare, part[:, :BL])

    placed = [0]

    def place_at(n):
        first = placed[0]
        placed[0] = first + PLACE[n]
        if PLACE[n]:
            lax.fori_loop(first, placed[0], place_rows, 0)

    def place_rows(k, _):
        first = pl.multiple_of(k * 256, 256)
        here = lax.broadcasted_iota(jnp.int32, (256, rows), 0) + first
        pick = (here == target).astype(F32).astype(BF)
        outgoing[pl.ds(first, 256), 0:width] = dot(pick, emb[...], 1, 0).astype(BF)
        outgoing[pl.ds(first, 256), width:] = dot(pick, digits, 1, 0).astype(BF)
        return 0

    place_at(0)
    pl.semaphore_wait(barrier, 10)

    half = packed.shape[0] // 2
    mine = pl.ds(pl.multiple_of(core * half, 8), half)
    other = pl.ds(pl.multiple_of((1 - core) * half, 8), half)
    swap = pltpu.make_async_remote_copy(
        src_ref=packed.at[other],
        dst_ref=half_in,
        send_sem=core_send,
        recv_sem=core_recv,
        device_id=sibling,
        device_id_type=MESH,
    )
    swap.start()

    place_at(1)
    swap.wait_recv()
    acc[...] = packed[mine, :] + half_in[...]

    def out_copy(d):
        rows_of = pl.ds(pl.multiple_of(d * SEND, SEND), SEND)
        return pltpu.make_async_remote_copy(
            src_ref=outgoing.at[rows_of, :],
            dst_ref=received.at[rows_of, :],
            send_sem=out_send,
            recv_sem=out_recv.at[d // (CHUNK // SEND)],
            device_id=chip_device(partner(d)),
            device_id_type=MESH,
        )

    sent_out = [1]

    def feed(count):
        first = sent_out[0]
        sent_out[0] = min(first + count, CHIPS)
        for d in range(first, sent_out[0]):
            out_copy(d).start()

    def ring_copy(stage, q, d, src, dst, device):
        return pltpu.make_async_remote_copy(
            src_ref=src,
            dst_ref=dst,
            send_sem=ring_send.at[stage * 9 + q * 3 + d - 1],
            recv_sem=ring_recv.at[stage * 9 + q * 3 + d - 1],
            device_id=device,
            device_id_type=MESH,
        )

    third = acc.shape[1] // 3
    cols = [slice(q * third, (q + 1) * third) for q in range(3)]
    axis_a = [AXES[q] for q in range(3)]
    axis_b = [AXES[(q + 1) % 3] for q in range(3)]
    axis_c = [AXES[(q + 2) % 3] for q in range(3)]
    sent = []
    stage1 = {}
    for d in (2, 1, 3):
        for q in range(3):
            device, to = axis_peer(axis_a[q], d)
            src = acc.at[pl.ds(pl.multiple_of(to * 64, 64), 64), cols[q]]
            c = ring_copy(0, q, d, src, in1.at[q, d - 1], device)
            c.start()
            stage1[q, d] = c
    place_at(2)
    feed(EARLY[1])
    stage2 = {}
    for q in range(3):
        for d in (1, 3, 2):
            stage1[q, d].wait_recv()
        a = place_on[axis_a[q]]
        own = acc[pl.ds(pl.multiple_of(a * 64, 64), 64), cols[q]]
        sum1[q] = (own + in1[q, 0]) + (in1[q, 1] + in1[q, 2])
        for d in (2, 1, 3):
            device, to = axis_peer(axis_b[q], d)
            src = sum1.at[q, pl.ds(pl.multiple_of(to * 16, 16), 16), :]
            c = ring_copy(1, q, d, src, in2.at[q, d - 1], device)
            c.start()
            stage2[q, d] = c
    place_at(3)
    feed(EARLY[2])
    stage3 = {}
    for q in range(3):
        for d in (1, 3, 2):
            stage2[q, d].wait_recv()
        b = place_on[axis_b[q]]
        c_at = place_on[axis_c[q]]
        own = sum1[q, pl.ds(pl.multiple_of(b * 16, 16), 16), :]
        in3[q, c_at] = (own + in2[q, 0]) + (in2[q, 1] + in2[q, 2])
        for d in (2, 1, 3):
            device, to = axis_peer(axis_c[q], d)
            c = ring_copy(2, q, d, in3.at[q, c_at], in3.at[q, c_at], device)
            c.start()
            stage3[q, d] = c
    place_at(4)
    feed(EARLY[3])
    stage4 = {}
    for q in range(3):
        for d in (1, 3, 2):
            stage3[q, d].wait_recv()
        a, b = place_on[axis_a[q]], place_on[axis_b[q]]
        there = pl.ds(pl.multiple_of(core * half + a * 64 + b * 16, 16), 16)
        total[there, cols[q]] = (in3[q, 0] + in3[q, 1]) + (in3[q, 2] + in3[q, 3])
        for d in (2, 1, 3):
            device, to = axis_peer(axis_b[q], d)
            c = ring_copy(3, q, d, total.at[there, cols[q]], total.at[there, cols[q]], device)
            c.start()
            stage4[q, d] = c
    place_at(5)
    feed(EARLY[4])
    stage5 = {}
    for q in range(3):
        for d in (1, 3, 2):
            stage4[q, d].wait_recv()
        a = place_on[axis_a[q]]
        there = pl.ds(pl.multiple_of(core * half + a * 64, 64), 64)
        for d in (2, 1, 3):
            device, to = axis_peer(axis_a[q], d)
            c = ring_copy(4, q, d, total.at[there, cols[q]], total.at[there, cols[q]], device)
            c.start()
            stage5[q, d] = c
    up = []
    for q in range(3):
        for d in (1, 3, 2):
            stage5[q, d].wait_recv()
        c = pltpu.make_async_remote_copy(
            src_ref=total.at[mine, cols[q]],
            dst_ref=total.at[mine, cols[q]],
            send_sem=up_send.at[q],
            recv_sem=up_recv.at[q],
            device_id=sibling,
            device_id_type=MESH,
        )
        c.start()
        up.append(c)

    keep = pltpu.make_async_copy(outgoing.at[0:SEND, :], received.at[0:SEND, :], out_recv.at[0])
    keep.start()
    for c in up:
        c.wait_recv()

    inv_n = 1.0 / doc_count
    center = []
    trace = jnp.zeros((BL, BL), F32)
    for i in range(8):
        r0, c0 = place(i)
        d = total[r0 : r0 + BL, c0 : c0 + BL]
        tail = d[BL - 8 :, :]
        c = jnp.where(lane[:1] < 64, tail[6:7], pltpu.roll(tail, 64, 1)[7:8]) * inv_n
        center.append(c)
        cb = jnp.broadcast_to(c, (BL, BL))
        trace = trace + jnp.where(lane == sub, d * inv_n - cb * cb, 0.0)
    trace = jnp.sum(jnp.sum(trace, axis=1, keepdims=True), axis=0, keepdims=True)
    ridge = 0.001 * trace * (1.0 / width)
    for i in range(8):
        r0, c0 = place(i)
        col = jnp.broadcast_to(center[i], (BL, BL)).T
        for j in range(i, 8):
            g = total[r0 : r0 + BL, c0 + (j - i) * BL : c0 + (j - i + 1) * BL]
            if j == i:
                g = jnp.where(lane >= sub, g, g.T)
            v = g * inv_n - col * center[j]
            if j == i:
                v = v + jnp.where(lane == sub, ridge, 0.0)
            mat[i * BL : (i + 1) * BL, j * BL : (j + 1) * BL] = v
        for j in range(i):
            mat[i * BL : (i + 1) * BL, j * BL : (j + 1) * BL] = jnp.zeros((BL, BL), F32)
    factor(mat, left_ref, right_ref, lambda p: feed(FEED_STEP) if p < FEED_STEPS else None)
    feed(CHIPS)
    shift = []
    for j in range(8):
        shift.append(
            dot_full(
                jnp.concatenate([jnp.broadcast_to(c, (8, BL)) for c in center[: j + 1]], axis=1),
                mat[j * BL : (j + 1) * BL, : (j + 1) * BL],
                1,
                1,
            )[0:1]
        )
    shift = jnp.concatenate(shift, axis=1)
    for i in range(8):
        for j in range(8):
            at = (slice(i * BL, (i + 1) * BL), slice(j * BL, (j + 1) * BL))
            if j <= i:
                v = mat[at]
                hi = v.astype(BF)
                w_hi[at] = hi
                w_lo[at] = (v - hi.astype(F32)).astype(BF)
            else:
                w_hi[at] = jnp.zeros((BL, BL), BF)
                w_lo[at] = jnp.zeros((BL, BL), BF)

    keys_half = received.shape[0]
    chunks = keys_half // CHUNK
    base = core * keys_half
    base_other = keys_half - base

    def chunk_of(first, k):
        return pl.ds(pl.multiple_of(first + k * CHUNK, CHUNK), CHUNK)

    def all_of(ref, sem):
        pltpu.make_async_copy(ref, ref, sem).wait()

    def pair_copy(k):
        there = chunk_of(base, k)
        return pltpu.make_async_remote_copy(
            src_ref=keys.at[there],
            dst_ref=keys.at[there],
            send_sem=pair_send.at[k],
            recv_sem=pair_recv.at[k],
            device_id=sibling,
            device_id_type=MESH,
        )

    def weights(shape, dim):
        i = lax.broadcasted_iota(jnp.int32, shape, dim)
        w = jnp.where(i == 0, 65536.0, jnp.where(i == 1, 256.0, jnp.where(i == 2, 1.0, 0.0)))
        return w.astype(BF)

    def rank_row(at):
        key_rank[:, at] = dot(weights((8, DIGITS), 1), keys[at, width:], 1, 1)

    def tile(q_at, k_at, row_ref, row_at, col_ref, col_at):
        scores = dot(keys[q_at, :width], keys[k_at, :width], 1, 1)
        q_rank = dot(keys[q_at, width:], weights((DIGITS, BL), 0), 1, 0)
        rank = key_rank[0:1, k_at]
        row = row_ref[row_at, :]
        cols = []
        for c in range(CHUNK // BL):
            at = slice(c * BL, (c + 1) * BL)
            earlier = rank[:, at] > q_rank
            row = jnp.maximum(row, jnp.where(earlier, scores[:, at], -1.0))
            if col_ref is not None:
                back = jnp.where(earlier, -1.0, scores[:, at])
                cols.append(jnp.max(back.reshape(CHUNK // 8, 8, BL), axis=0))
        row_ref[row_at, :] = row
        if col_ref is not None:
            col_ref[:, col_at] = jnp.maximum(col_ref[:, col_at], jnp.concatenate(cols, axis=1))

    row_best[...] = jnp.full(row_best.shape, -1.0, F32)
    col_best[...] = jnp.full(col_best.shape, -1.0, F32)
    cross_row[...] = jnp.full(cross_row.shape, -1.0, F32)
    cross_col[...] = jnp.full(cross_col.shape, -1.0, F32)

    def chunk_step(k, _):
        here = chunk_of(0, k)
        all_of(received.at[here, :], out_recv.at[k])
        there = chunk_of(base, k)
        parts = []
        norm = jnp.zeros((CHUNK, 1), F32)
        for j in range(4):
            deep = 256 * (j + 1)
            a = received[here, :deep]
            out = slice(256 * j, deep)
            p = dot(a, w_hi[out, :deep], 1, 1) + dot(a, w_lo[out, :deep], 1, 1) - shift[:, out]
            parts.append(p)
            norm = norm + jnp.sum(p * p, axis=1, keepdims=True)
        scale = lax.rsqrt(norm + 1e-06)
        for j in range(4):
            keys[there, 256 * j : 256 * j + 256] = (parts[j] * scale).astype(BF)
        keys[there, width:] = received[here, width:]
        pair_copy(k).start()
        rank_row(there)

        def own(a, _):
            tile(chunk_of(base, a), there, row_best, chunk_of(0, a), col_best, here)
            return 0

        lax.fori_loop(0, k, own, 0)
        tile(there, there, row_best, here, None, None)
        pair_copy(k).wait_recv()
        rank_row(chunk_of(base_other, k))
        j0 = (k + core) % 2
        n1 = (k - j0 + 2) // 2
        n2 = (k - j0 + 1) // 2

        def cross(u, _):
            i = jnp.where(u < n1, k, j0 + 2 * (u - n1))
            j = jnp.where(u < n1, j0 + 2 * u, k)
            tile(chunk_of(0, i), chunk_of(keys_half, j), cross_row, chunk_of(0, i), cross_col, chunk_of(0, j))
            return 0

        lax.fori_loop(0, n1 + n2, cross, 0)
        return 0

    lax.fori_loop(0, chunks, chunk_step, 0)

    def line_of(ref, g):
        return jnp.max(ref[g * BL : (g + 1) * BL, :].T, axis=0, keepdims=True)

    groups = keys_half // BL
    for g in range(groups):
        at = slice(g * BL, (g + 1) * BL)
        cross_out[g : g + 1, :] = line_of(cross_row, g)
        cross_out[groups + g : groups + g + 1, :] = jnp.max(cross_col[:, at], axis=0, keepdims=True)
    share = pltpu.make_async_remote_copy(
        src_ref=cross_out,
        dst_ref=cross_in,
        send_sem=share_send,
        recv_sem=share_recv,
        device_id=sibling,
        device_id_type=MESH,
    )
    share.start()
    lines = []
    for g in range(groups):
        at = slice(g * BL, (g + 1) * BL)
        lines.append(jnp.maximum(line_of(row_best, g), jnp.max(col_best[:, at], axis=0, keepdims=True)))
    lines = jnp.concatenate(lines, axis=0)
    share.wait_recv()
    both = jnp.maximum(cross_out[...], cross_in[...])
    lines = jnp.maximum(lines, jnp.where(core == 0, both[:groups], both[groups:]))
    for g in range(groups):
        ret_out[g] = bcast(lines[g : g + 1, :])

    def ret_copy(d):
        return pltpu.make_async_remote_copy(
            src_ref=ret_out.at[d // 4],
            dst_ref=ret_in.at[d],
            send_sem=ret_send,
            recv_sem=ret_recv,
            device_id=chip_device(source(d)),
            device_id_type=MESH,
        )

    for d in range(1, CHIPS):
        ret_copy(d).start()
    ret_in[0] = ret_out[0]
    picks = member.astype(F32).astype(BF)
    at_lane = lax.broadcasted_iota(jnp.int32, (BL, rows), 0) == slot + SEND * (label % 4)

    swap.wait_send()
    share.wait_send()
    for stage in (stage1, stage2, stage3, stage4, stage5):
        for c in stage.values():
            c.wait_send()
    for c in up:
        c.wait_send()

    all_of(outgoing.at[SEND:, :], out_send)
    for k in range(chunks):
        pair_copy(k).wait_send()
    all_of(ret_in.at[1:], ret_recv)
    all_of(ret_in.at[1:], ret_send)
    table = ret_in[:, 0, :]
    hi = table.astype(BF)
    rest = table - hi.astype(F32)
    mid = rest.astype(BF)
    low = (rest - mid.astype(F32)).astype(BF)
    mine_of = dot(hi, picks, 0, 0) + (dot(mid, picks, 0, 0) + dot(low, picks, 0, 0))
    out_ref[...] = jnp.sum(jnp.where(at_lane, mine_of, 0.0), axis=0, keepdims=True)


def per_device(embeddings, clusters, doc_order):
    rows, width = embeddings.shape
    doc_count = rows * lax.axis_size("dp") * lax.axis_size("help")
    slots = CHIPS * SEND
    wide = width + DIGITS
    dma = pltpu.SemaphoreType.DMA
    vmem = pltpu.VMEM
    out = pl.pallas_call(
        lambda *refs: kernel(doc_count, *refs),
        out_shape=jax.ShapeDtypeStruct((1, rows), F32),
        in_specs=[
            pl.BlockSpec(memory_space=pl.ANY),
            pl.BlockSpec(memory_space=pltpu.VMEM),
            pl.BlockSpec(memory_space=pltpu.VMEM),
        ],
        out_specs=pl.BlockSpec(memory_space=pltpu.VMEM),
        scratch_shapes=[
            vmem((rows, width), BF),
            vmem((slots, wide), BF),
            vmem((slots, wide), BF),
            vmem((2 * slots, wide), BF),
            vmem((512, 1152), F32),
            vmem((256, 1152), F32),
            vmem((256, 1152), F32),
            vmem((3, 3, 64, 384), F32),
            vmem((3, 64, 384), F32),
            vmem((3, 3, 16, 384), F32),
            vmem((3, 4, 16, 384), F32),
            vmem((512, 1152), F32),
            vmem((width, width), F32),
            vmem((6 * BL, width), BF),
            vmem((6 * BL, width), BF),
            vmem((width, width), BF),
            vmem((width, width), BF),
            vmem((8, 2 * slots), F32),
            vmem((slots, BL), F32),
            vmem((8, slots), F32),
            vmem((slots, BL), F32),
            vmem((8, slots), F32),
            vmem((32, BL), F32),
            vmem((32, BL), F32),
            vmem((16, 8, BL), F32),
            vmem((CHIPS, 8, BL), F32),
            dma,
            dma,
            dma,
            dma((45,)),
            dma((45,)),
            dma((3,)),
            dma((3,)),
            dma,
            dma((slots // CHUNK,)),
            dma((slots // CHUNK,)),
            dma((slots // CHUNK,)),
            dma,
            dma,
            dma,
            dma,
        ],
        compiler_params=pltpu.CompilerParams(
            collective_id=0, has_side_effects=True, vmem_limit_bytes=56 * 2**20
        ),
    )(embeddings, clusters.reshape(1, rows), doc_order.reshape(1, rows))
    return out.reshape(rows)


def solution(mesh):
    in_specs = (P(("dp", "help"), None), P(("dp", "help")), P(("dp", "help")))
    out_specs = P(("dp", "help"))
    return jax.shard_map(
        per_device, mesh=mesh, in_specs=in_specs, out_specs=out_specs, check_vma=False
    )
```

```python
import jax
import jax.numpy as jnp
from jax import lax
from jax.experimental import pallas as pl
from jax.experimental.pallas import tpu as pltpu
from jax.sharding import PartitionSpec as P

F32 = jnp.float32
BF = jnp.bfloat16
MESH = pl.DeviceIdType.MESH
BL = 128
SEND = 32
CHIPS = 64
DIGITS = 128
AXES = ("x", "y", "z")
PLACE = (0, 2, 3, 1, 1, 1)
EARLY = (0, 0, 0, 0, 4)
FEED_STEP = 16
MIX, UNMIX = 45, 37
CHUNK = 512
FEED_STEPS = 8


def dot(a, b, ca, cb):
    return lax.dot_general(a, b, (((ca,), (cb,)), ((), ())), preferred_element_type=F32)


def dot_full(a, b, ca, cb):
    return lax.dot_general(
        a,
        b,
        (((ca,), (cb,)), ((), ())),
        precision=lax.Precision.HIGHEST,
        preferred_element_type=F32,
    )


def bcast(v):
    return jnp.broadcast_to(v, (8, BL))


def sum_tree(x):
    while len(x) > 1:
        x = [x[i] + x[i + 1] for i in range(0, len(x), 2)]
    return x[0]


def split3(v):
    hi = v.astype(BF)
    rest = v - hi.astype(F32)
    mid = rest.astype(BF)
    return hi, mid, (rest - mid.astype(F32)).astype(BF)


LEFT = (0, 0, 1, 0, 2, 1)
RIGHT = (0, 1, 0, 2, 0, 1)


def stack(parts, order, axis):
    return jnp.concatenate([parts[n] for n in order], axis=axis)


GROUP = 8


def lanes(v, first):
    return [bcast(v[:, first + k : first + k + 1]) for k in range(8)]


def combine(m, v):
    return sum_tree([m[k] * bcast(v[k : k + 1]) for k in range(8)])


def chol_inverse_block(rows, between):
    sub = lax.broadcasted_iota(jnp.int32, (8, BL), 0)
    lane = lax.broadcasted_iota(jnp.int32, (8, BL), 1)
    rows = list(rows)
    out = []
    for g in range(16 // GROUP):
        norm = []
        end = GROUP * (g + 1)
        cols = lanes(rows[GROUP * g], 8 * GROUP * g)
        for p in range(GROUP * g, end):
            inside = (lane >= 8 * p) & (lane < 8 * p + 8)
            r = jnp.where(inside, jnp.where(lane == sub + 8 * p, 1.0, 0.0), rows[p])
            tf = r
            scale = jnp.zeros((8, BL), F32)
            later = lanes(rows[p], 8 * p + 8) if p + 1 < end else []
            invs = []
            for j in range(8):
                d = bcast(cols[j][j : j + 1])
                inv = 1.0 / d
                invs.append(inv)
                scale = jnp.where(sub == j, d, scale)
                times = jnp.where(sub == j, 0.0, cols[j]) * inv
                tf = tf - jnp.where(sub > j, times, 0.0) * bcast(tf[j : j + 1])
                for k in range(j + 1, 8):
                    cols[k] = cols[k] - times * bcast(cols[k][j : j + 1])
                r = r - times * bcast(r[j : j + 1])
                later = [v - times * bcast(v[j : j + 1]) for v in later]
            norm.append(tf * lax.rsqrt(scale))
            for i in range(p + 1, end):
                m = [v * invs[k] for k, v in enumerate(lanes(rows[i], 8 * p))]
                if i == p + 1:
                    pivots = lanes(rows[i], 8 * i)
                    cols = [pivots[k] - combine(m, later[k]) for k in range(8)]
                rows[i] = jnp.where(inside, 0.0, rows[i]) - combine(m, r)
            out.append(jnp.where(lane < 8 * p + 8, norm[-1], 0.0))
            between(p)
        if end < 16:
            for q in range(GROUP):
                p = GROUP * g + q
                norm[q] = jnp.where((lane >= 8 * p + 8) & (lane < 8 * end), 0.0, norm[q])
            parts = split3(jnp.concatenate(norm, axis=0))
            gone = dot(stack(parts, LEFT, 0), stack(parts, RIGHT, 0), 0, 0)
            mine = (lane >= 8 * GROUP * g) & (lane < 8 * end)
            for i in range(end, 16):
                rows[i] = jnp.where(mine, 0.0, rows[i]) - gone[8 * i : 8 * i + 8, :]
    return jnp.concatenate(out, axis=0)


def factor(m_ref, left_ref, right_ref, feed, terms=6):
    n = m_ref.shape[0]
    blocks = n // BL
    left_order, right_order = LEFT[:terms], RIGHT[:terms]

    def cut(i):
        return slice(i * BL, (i + 1) * BL)

    def deferred(p, w_stack):
        def rest_of_row(c0, c1):
            def go():
                parts = split3(m_ref[cut(p), c0:c1])
                r = dot(w_stack, stack(parts, right_order, 0), 1, 0)
                m_ref[cut(p), c0:c1] = r
                parts = split3(r)
                left_ref[:, c0:c1] = stack(parts, left_order, 0)
                right_ref[:, c0:c1] = stack(parts, right_order, 0)
            return go
        def trail(i):
            def go():
                lhs = left_ref[:, cut(i)]
                m_ref[cut(i), cut(p)] = jnp.zeros((BL, BL), F32)
                low = slice(0, (p + 1) * BL)
                m_ref[cut(i), low] = m_ref[cut(i), low] - dot(lhs, right_ref[:, low], 0, 0)
                first = i + 1 if i == p + 1 else i
                if first < blocks:
                    up = slice(first * BL, n)
                    m_ref[cut(i), up] = m_ref[cut(i), up] - dot(lhs, right_ref[:, up], 0, 0)
            return go
        todo = []
        if p > 0:
            todo.append(rest_of_row(0, p * BL))
        if p + 2 < blocks:
            todo.append(rest_of_row((p + 2) * BL, n))
        return todo + [trail(i) for i in range(p + 1, blocks)]

    todo = []
    for p in range(blocks):
        feed(p)
        count = len(todo)
        done = [0]

        def between(q):
            upto = -(-count * (q + 1) // 13)
            while done[0] < min(upto, count):
                todo[done[0]]()
                done[0] += 1

        w = chol_inverse_block([m_ref[p * BL + 8 * i : p * BL + 8 * i + 8, cut(p)] for i in range(16)], between)
        w_parts = split3(w)
        w_stack = stack(w_parts, left_order, 1)
        if p + 1 < blocks:
            nxt = cut(p + 1)
            parts = split3(m_ref[cut(p), nxt])
            r = dot(w_stack, stack(parts, right_order, 0), 1, 0)
            m_ref[cut(p), nxt] = r
            parts = split3(r)
            lhs, rhs = stack(parts, left_order, 0), stack(parts, right_order, 0)
            left_ref[:, nxt] = lhs
            right_ref[:, nxt] = rhs
            m_ref[nxt, nxt] = m_ref[nxt, nxt] - dot(lhs, rhs, 0, 0)
            left_ref[:, cut(p)] = stack(w_parts, left_order, 0)
            right_ref[:, cut(p)] = stack(w_parts, right_order, 0)
        elif p > 0:
            parts = split3(m_ref[cut(p), : p * BL])
            m_ref[cut(p), : p * BL] = dot(w_stack, stack(parts, right_order, 0), 1, 0)
        m_ref[cut(p), cut(p)] = w
        todo = deferred(p, w_stack)


def place(i):
    return min(i, 7 - i) * BL, 0 if i < 4 else (i + 1) * BL


def slots_of(clusters_row):
    n = clusters_row.shape[1]
    member = lax.broadcasted_iota(jnp.int32, (CHIPS, n), 0) == clusters_row
    before = lax.broadcasted_iota(jnp.int32, (n, n), 0) < lax.broadcasted_iota(jnp.int32, (n, n), 1)
    count = dot(member.astype(F32).astype(BF), before.astype(F32).astype(BF), 1, 0)
    slot = jnp.sum(jnp.where(member, count, 0.0), axis=0, keepdims=True)
    return member, slot.astype(jnp.int32)


def digits_of(order_row, doc_count):
    n = order_row.shape[1]
    value = doc_count - order_row
    row = lax.broadcasted_iota(jnp.int32, (DIGITS, n), 0)
    d = jnp.where(row == 0, value >> 16, jnp.where(row == 1, (value >> 8) & 255, value & 255))
    return jnp.where(row < 3, d, 0).astype(F32).T.astype(BF)


def kernel(
    doc_count,
    emb_ref,
    clusters_ref,
    order_ref,
    out_ref,
    emb,
    outgoing,
    received,
    keys,
    packed,
    half_in,
    acc,
    in1,
    sum1,
    in2,
    in3,
    total,
    mat,
    left_ref,
    right_ref,
    w_hi,
    w_lo,
    key_rank,
    row_best,
    col_best,
    cross_row,
    cross_col,
    cross_out,
    cross_in,
    ret_out,
    ret_in,
    emb_sem,
    core_send,
    core_recv,
    ring_send,
    ring_recv,
    up_send,
    up_recv,
    out_send,
    out_recv,
    pair_send,
    pair_recv,
    share_send,
    share_recv,
    ret_send,
    ret_recv,
):
    dp = lax.axis_index("dp")
    y = lax.axis_index("help")
    core = dp % 2
    x = dp // 8
    z = (dp // 2) % 4
    chip = (dp // 2) * 4 + y
    sibling = (dp + 1 - 2 * core, y)
    rows = emb.shape[0]
    width = emb.shape[1]

    def chip_device(c):
        return ((c >> 2) * 2 + core, c & 3)

    sign = 1 - 2 * core

    def chip_at(dx, dy, dz):
        return (((x + dx) & 3) * 4 + ((z + dz) & 3)) * 4 + ((y + dy) & 3)

    def partner(d):
        d = d * MIX % CHIPS
        return chip_at(sign * (d // 16), sign * (d % 4), sign * (d // 4 % 4))

    def source(d):
        d = d * MIX % CHIPS
        return chip_at(-sign * (d // 16), -sign * (d % 4), -sign * (d // 4 % 4))

    def axis_peer(axis, d):
        if axis == "x":
            to = (x + d) % 4
            return ((to * 4 + z) * 2 + core, y), to
        if axis == "z":
            to = (z + d) % 4
            return ((x * 4 + to) * 2 + core, y), to
        to = (y + d) % 4
        return (dp, to), to

    place_on = {"x": x, "y": y, "z": z}

    barrier = pltpu.get_barrier_semaphore()

    for axis in AXES:
        for d in (1, 2, 3):
            device, _ = axis_peer(axis, d)
            pl.semaphore_signal(barrier, inc=1, device_id=device, device_id_type=MESH)
    pl.semaphore_signal(barrier, inc=1, device_id=sibling, device_id_type=MESH)
    load = pltpu.make_async_copy(emb_ref, emb, emb_sem)
    load.start()
    label = clusters_ref[...]
    label = (
        (((label >> 4) - x) * sign & 3) * 16
        + (((label >> 2 & 3) - z) * sign & 3) * 4
        + (((label & 3) - y) * sign & 3)
    ) * UNMIX & (CHIPS - 1)
    member, slot = slots_of(label)
    target = label * SEND + slot
    digits = digits_of(order_ref[...], doc_count)
    load.wait()

    col_sum = dot(jnp.ones((8, rows), BF), emb[...], 1, 0)
    sub = lax.broadcasted_iota(jnp.int32, (BL, BL), 0)
    lane = lax.broadcasted_iota(jnp.int32, (BL, BL), 1)
    for b in range(width // 256):
        block = dot(emb[:, 256 * b : 256 * b + 256], emb[:, 256 * b :], 0, 0)
        for i in (2 * b, 2 * b + 1):
            r0, c0 = place(i)
            skip = (i - 2 * b) * BL
            part = block[skip : skip + BL, skip:]
            w = part.shape[1]
            packed[r0 : r0 + BL, c0 : c0 + w] = part
            cs = jnp.broadcast_to(col_sum[0:1, i * BL : i * BL + BL], (BL, BL))
            spare = jnp.where(sub == BL - 2, cs, pltpu.roll(cs, 64, 1))
            use = (sub >= BL - 2) & (lane < 64)
            packed[r0 : r0 + BL, c0 : c0 + BL] = jnp.where(use, spare, part[:, :BL])

    placed = [0]

    def place_at(n):
        first = placed[0]
        placed[0] = first + PLACE[n]
        if PLACE[n]:
            lax.fori_loop(first, placed[0], place_rows, 0)

    def place_rows(k, _):
        first = pl.multiple_of(k * 256, 256)
        here = lax.broadcasted_iota(jnp.int32, (256, rows), 0) + first
        pick = (here == target).astype(F32).astype(BF)
        outgoing[pl.ds(first, 256), 0:width] = dot(pick, emb[...], 1, 0).astype(BF)
        outgoing[pl.ds(first, 256), width:] = dot(pick, digits, 1, 0).astype(BF)
        return 0

    place_at(0)
    pl.semaphore_wait(barrier, 10)

    half = packed.shape[0] // 2
    mine = pl.ds(pl.multiple_of(core * half, 8), half)
    other = pl.ds(pl.multiple_of((1 - core) * half, 8), half)
    swap = pltpu.make_async_remote_copy(
        src_ref=packed.at[other],
        dst_ref=half_in,
        send_sem=core_send,
        recv_sem=core_recv,
        device_id=sibling,
        device_id_type=MESH,
    )
    swap.start()

    place_at(1)
    swap.wait_recv()
    acc[...] = packed[mine, :] + half_in[...]

    def out_copy(d):
        rows_of = pl.ds(pl.multiple_of(d * SEND, SEND), SEND)
        return pltpu.make_async_remote_copy(
            src_ref=outgoing.at[rows_of, :],
            dst_ref=received.at[rows_of, :],
            send_sem=out_send,
            recv_sem=out_recv.at[d // (CHUNK // SEND)],
            device_id=chip_device(partner(d)),
            device_id_type=MESH,
        )

    sent_out = [1]

    def feed(count):
        first = sent_out[0]
        sent_out[0] = min(first + count, CHIPS)
        for d in range(first, sent_out[0]):
            out_copy(d).start()

    def ring_copy(stage, q, d, src, dst, device):
        return pltpu.make_async_remote_copy(
            src_ref=src,
            dst_ref=dst,
            send_sem=ring_send.at[stage * 9 + q * 3 + d - 1],
            recv_sem=ring_recv.at[stage * 9 + q * 3 + d - 1],
            device_id=device,
            device_id_type=MESH,
        )

    third = acc.shape[1] // 3
    cols = [slice(q * third, (q + 1) * third) for q in range(3)]
    axis_a = [AXES[q] for q in range(3)]
    axis_b = [AXES[(q + 1) % 3] for q in range(3)]
    axis_c = [AXES[(q + 2) % 3] for q in range(3)]
    sent = []
    stage1 = {}
    for d in (2, 1, 3):
        for q in range(3):
            device, to = axis_peer(axis_a[q], d)
            src = acc.at[pl.ds(pl.multiple_of(to * 64, 64), 64), cols[q]]
            c = ring_copy(0, q, d, src, in1.at[q, d - 1], device)
            c.start()
            stage1[q, d] = c
    place_at(2)
    feed(EARLY[1])
    stage2 = {}
    for q in range(3):
        for d in (1, 3, 2):
            stage1[q, d].wait_recv()
        a = place_on[axis_a[q]]
        own = acc[pl.ds(pl.multiple_of(a * 64, 64), 64), cols[q]]
        sum1[q] = (own + in1[q, 0]) + (in1[q, 1] + in1[q, 2])
        for d in (2, 1, 3):
            device, to = axis_peer(axis_b[q], d)
            src = sum1.at[q, pl.ds(pl.multiple_of(to * 16, 16), 16), :]
            c = ring_copy(1, q, d, src, in2.at[q, d - 1], device)
            c.start()
            stage2[q, d] = c
    place_at(3)
    feed(EARLY[2])
    stage3 = {}
    for q in range(3):
        for d in (1, 3, 2):
            stage2[q, d].wait_recv()
        b = place_on[axis_b[q]]
        c_at = place_on[axis_c[q]]
        own = sum1[q, pl.ds(pl.multiple_of(b * 16, 16), 16), :]
        in3[q, c_at] = (own + in2[q, 0]) + (in2[q, 1] + in2[q, 2])
        for d in (2, 1, 3):
            device, to = axis_peer(axis_c[q], d)
            c = ring_copy(2, q, d, in3.at[q, c_at], in3.at[q, c_at], device)
            c.start()
            stage3[q, d] = c
    place_at(4)
    feed(EARLY[3])
    stage4 = {}
    for q in range(3):
        for d in (1, 3, 2):
            stage3[q, d].wait_recv()
        a, b = place_on[axis_a[q]], place_on[axis_b[q]]
        there = pl.ds(pl.multiple_of(core * half + a * 64 + b * 16, 16), 16)
        total[there, cols[q]] = (in3[q, 0] + in3[q, 1]) + (in3[q, 2] + in3[q, 3])
        for d in (2, 1, 3):
            device, to = axis_peer(axis_b[q], d)
            c = ring_copy(3, q, d, total.at[there, cols[q]], total.at[there, cols[q]], device)
            c.start()
            stage4[q, d] = c
    place_at(5)
    feed(EARLY[4])
    stage5 = {}
    for q in range(3):
        for d in (1, 3, 2):
            stage4[q, d].wait_recv()
        a = place_on[axis_a[q]]
        there = pl.ds(pl.multiple_of(core * half + a * 64, 64), 64)
        for d in (2, 1, 3):
            device, to = axis_peer(axis_a[q], d)
            c = ring_copy(4, q, d, total.at[there, cols[q]], total.at[there, cols[q]], device)
            c.start()
            stage5[q, d] = c
    up = []
    for q in range(3):
        for d in (1, 3, 2):
            stage5[q, d].wait_recv()
        c = pltpu.make_async_remote_copy(
            src_ref=total.at[mine, cols[q]],
            dst_ref=total.at[mine, cols[q]],
            send_sem=up_send.at[q],
            recv_sem=up_recv.at[q],
            device_id=sibling,
            device_id_type=MESH,
        )
        c.start()
        up.append(c)

    keep = pltpu.make_async_copy(outgoing.at[0:SEND, :], received.at[0:SEND, :], out_recv.at[0])
    keep.start()
    for c in up:
        c.wait_recv()

    inv_n = 1.0 / doc_count
    center = []
    trace = jnp.zeros((BL, BL), F32)
    for i in range(8):
        r0, c0 = place(i)
        d = total[r0 : r0 + BL, c0 : c0 + BL]
        tail = d[BL - 8 :, :]
        c = jnp.where(lane[:1] < 64, tail[6:7], pltpu.roll(tail, 64, 1)[7:8]) * inv_n
        center.append(c)
        cb = jnp.broadcast_to(c, (BL, BL))
        trace = trace + jnp.where(lane == sub, d * inv_n - cb * cb, 0.0)
    trace = jnp.sum(jnp.sum(trace, axis=1, keepdims=True), axis=0, keepdims=True)
    ridge = 0.001 * trace * (1.0 / width)
    for i in range(8):
        r0, c0 = place(i)
        col = jnp.broadcast_to(center[i], (BL, BL)).T
        for j in range(i, 8):
            g = total[r0 : r0 + BL, c0 + (j - i) * BL : c0 + (j - i + 1) * BL]
            if j == i:
                g = jnp.where(lane >= sub, g, g.T)
            v = g * inv_n - col * center[j]
            if j == i:
                v = v + jnp.where(lane == sub, ridge, 0.0)
            mat[i * BL : (i + 1) * BL, j * BL : (j + 1) * BL] = v
        for j in range(i):
            mat[i * BL : (i + 1) * BL, j * BL : (j + 1) * BL] = jnp.zeros((BL, BL), F32)
    factor(mat, left_ref, right_ref, lambda p: feed(FEED_STEP) if p < FEED_STEPS else None)
    feed(CHIPS)
    shift = []
    for j in range(8):
        shift.append(
            dot_full(
                jnp.concatenate([jnp.broadcast_to(c, (8, BL)) for c in center[: j + 1]], axis=1),
                mat[j * BL : (j + 1) * BL, : (j + 1) * BL],
                1,
                1,
            )[0:1]
        )
    shift = jnp.concatenate(shift, axis=1)
    for i in range(8):
        for j in range(8):
            at = (slice(i * BL, (i + 1) * BL), slice(j * BL, (j + 1) * BL))
            if j <= i:
                v = mat[at]
                hi = v.astype(BF)
                w_hi[at] = hi
                w_lo[at] = (v - hi.astype(F32)).astype(BF)
            else:
                w_hi[at] = jnp.zeros((BL, BL), BF)
                w_lo[at] = jnp.zeros((BL, BL), BF)

    keys_half = received.shape[0]
    chunks = keys_half // CHUNK
    base = core * keys_half
    base_other = keys_half - base

    def chunk_of(first, k):
        return pl.ds(pl.multiple_of(first + k * CHUNK, CHUNK), CHUNK)

    def all_of(ref, sem):
        pltpu.make_async_copy(ref, ref, sem).wait()

    def pair_copy(k):
        there = chunk_of(base, k)
        return pltpu.make_async_remote_copy(
            src_ref=keys.at[there],
            dst_ref=keys.at[there],
            send_sem=pair_send.at[k],
            recv_sem=pair_recv.at[k],
            device_id=sibling,
            device_id_type=MESH,
        )

    def weights(shape, dim):
        i = lax.broadcasted_iota(jnp.int32, shape, dim)
        w = jnp.where(i == 0, 65536.0, jnp.where(i == 1, 256.0, jnp.where(i == 2, 1.0, 0.0)))
        return w.astype(BF)

    def rank_row(at):
        key_rank[:, at] = dot(weights((8, DIGITS), 1), keys[at, width:], 1, 1)

    def tile(q_at, k_at, row_ref, row_at, col_ref, col_at):
        scores = dot(keys[q_at, :width], keys[k_at, :width], 1, 1)
        q_rank = dot(keys[q_at, width:], weights((DIGITS, BL), 0), 1, 0)
        rank = key_rank[0:1, k_at]
        row = row_ref[row_at, :]
        cols = []
        for c in range(CHUNK // BL):
            at = slice(c * BL, (c + 1) * BL)
            earlier = rank[:, at] > q_rank
            row = jnp.maximum(row, jnp.where(earlier, scores[:, at], -1.0))
            if col_ref is not None:
                back = jnp.where(earlier, -1.0, scores[:, at])
                cols.append(jnp.max(back.reshape(CHUNK // 8, 8, BL), axis=0))
        row_ref[row_at, :] = row
        if col_ref is not None:
            col_ref[:, col_at] = jnp.maximum(col_ref[:, col_at], jnp.concatenate(cols, axis=1))

    row_best[...] = jnp.full(row_best.shape, -1.0, F32)
    col_best[...] = jnp.full(col_best.shape, -1.0, F32)
    cross_row[...] = jnp.full(cross_row.shape, -1.0, F32)
    cross_col[...] = jnp.full(cross_col.shape, -1.0, F32)

    def chunk_step(k, _):
        here = chunk_of(0, k)
        all_of(received.at[here, :], out_recv.at[k])
        there = chunk_of(base, k)
        parts = []
        norm = jnp.zeros((CHUNK, 1), F32)
        for j in range(4):
            deep = 256 * (j + 1)
            a = received[here, :deep]
            out = slice(256 * j, deep)
            p = dot(a, w_hi[out, :deep], 1, 1) + dot(a, w_lo[out, :deep], 1, 1) - shift[:, out]
            parts.append(p)
            norm = norm + jnp.sum(p * p, axis=1, keepdims=True)
        scale = lax.rsqrt(norm + 1e-06)
        for j in range(4):
            keys[there, 256 * j : 256 * j + 256] = (parts[j] * scale).astype(BF)
        keys[there, width:] = received[here, width:]
        pair_copy(k).start()
        rank_row(there)

        def own(a, _):
            tile(chunk_of(base, a), there, row_best, chunk_of(0, a), col_best, here)
            return 0

        lax.fori_loop(0, k, own, 0)
        tile(there, there, row_best, here, None, None)
        pair_copy(k).wait_recv()
        rank_row(chunk_of(base_other, k))
        j0 = (k + core) % 2
        n1 = (k - j0 + 2) // 2
        n2 = (k - j0 + 1) // 2

        def cross(u, _):
            i = jnp.where(u < n1, k, j0 + 2 * (u - n1))
            j = jnp.where(u < n1, j0 + 2 * u, k)
            tile(chunk_of(0, i), chunk_of(keys_half, j), cross_row, chunk_of(0, i), cross_col, chunk_of(0, j))
            return 0

        lax.fori_loop(0, n1 + n2, cross, 0)
        return 0

    lax.fori_loop(0, chunks, chunk_step, 0)

    def line_of(ref, g):
        return jnp.max(ref[g * BL : (g + 1) * BL, :].T, axis=0, keepdims=True)

    groups = keys_half // BL
    for g in range(groups):
        at = slice(g * BL, (g + 1) * BL)
        cross_out[g : g + 1, :] = line_of(cross_row, g)
        cross_out[groups + g : groups + g + 1, :] = jnp.max(cross_col[:, at], axis=0, keepdims=True)
    share = pltpu.make_async_remote_copy(
        src_ref=cross_out,
        dst_ref=cross_in,
        send_sem=share_send,
        recv_sem=share_recv,
        device_id=sibling,
        device_id_type=MESH,
    )
    share.start()
    lines = []
    for g in range(groups):
        at = slice(g * BL, (g + 1) * BL)
        lines.append(jnp.maximum(line_of(row_best, g), jnp.max(col_best[:, at], axis=0, keepdims=True)))
    lines = jnp.concatenate(lines, axis=0)
    share.wait_recv()
    both = jnp.maximum(cross_out[...], cross_in[...])
    lines = jnp.maximum(lines, jnp.where(core == 0, both[:groups], both[groups:]))
    for g in range(groups):
        ret_out[g] = bcast(lines[g : g + 1, :])

    def ret_copy(d):
        return pltpu.make_async_remote_copy(
            src_ref=ret_out.at[d // 4],
            dst_ref=ret_in.at[d],
            send_sem=ret_send,
            recv_sem=ret_recv,
            device_id=chip_device(source(d)),
            device_id_type=MESH,
        )

    for d in range(1, CHIPS):
        ret_copy(d).start()
    ret_in[0] = ret_out[0]
    picks = member.astype(F32).astype(BF)
    at_lane = lax.broadcasted_iota(jnp.int32, (BL, rows), 0) == slot + SEND * (label % 4)

    swap.wait_send()
    share.wait_send()
    for stage in (stage1, stage2, stage3, stage4, stage5):
        for c in stage.values():
            c.wait_send()
    for c in up:
        c.wait_send()

    all_of(outgoing.at[SEND:, :], out_send)
    for k in range(chunks):
        pair_copy(k).wait_send()
    all_of(ret_in.at[1:], ret_recv)
    all_of(ret_in.at[1:], ret_send)
    table = ret_in[:, 0, :]
    hi = table.astype(BF)
    rest = table - hi.astype(F32)
    mid = rest.astype(BF)
    low = (rest - mid.astype(F32)).astype(BF)
    mine_of = dot(hi, picks, 0, 0) + (dot(mid, picks, 0, 0) + dot(low, picks, 0, 0))
    out_ref[...] = jnp.sum(jnp.where(at_lane, mine_of, 0.0), axis=0, keepdims=True)


def per_device(embeddings, clusters, doc_order):
    rows, width = embeddings.shape
    doc_count = rows * lax.axis_size("dp") * lax.axis_size("help")
    slots = CHIPS * SEND
    wide = width + DIGITS
    dma = pltpu.SemaphoreType.DMA
    vmem = pltpu.VMEM
    out = pl.pallas_call(
        lambda *refs: kernel(doc_count, *refs),
        out_shape=jax.ShapeDtypeStruct((1, rows), F32),
        in_specs=[
            pl.BlockSpec(memory_space=pl.ANY),
            pl.BlockSpec(memory_space=pltpu.VMEM),
            pl.BlockSpec(memory_space=pltpu.VMEM),
        ],
        out_specs=pl.BlockSpec(memory_space=pltpu.VMEM),
        scratch_shapes=[
            vmem((rows, width), BF),
            vmem((slots, wide), BF),
            vmem((slots, wide), BF),
            vmem((2 * slots, wide), BF),
            vmem((512, 1152), F32),
            vmem((256, 1152), F32),
            vmem((256, 1152), F32),
            vmem((3, 3, 64, 384), F32),
            vmem((3, 64, 384), F32),
            vmem((3, 3, 16, 384), F32),
            vmem((3, 4, 16, 384), F32),
            vmem((512, 1152), F32),
            vmem((width, width), F32),
            vmem((6 * BL, width), BF),
            vmem((6 * BL, width), BF),
            vmem((width, width), BF),
            vmem((width, width), BF),
            vmem((8, 2 * slots), F32),
            vmem((slots, BL), F32),
            vmem((8, slots), F32),
            vmem((slots, BL), F32),
            vmem((8, slots), F32),
            vmem((32, BL), F32),
            vmem((32, BL), F32),
            vmem((16, 8, BL), F32),
            vmem((CHIPS, 8, BL), F32),
            dma,
            dma,
            dma,
            dma((45,)),
            dma((45,)),
            dma((3,)),
            dma((3,)),
            dma,
            dma((slots // CHUNK,)),
            dma((slots // CHUNK,)),
            dma((slots // CHUNK,)),
            dma,
            dma,
            dma,
            dma,
        ],
        compiler_params=pltpu.CompilerParams(
            collective_id=0, has_side_effects=True, vmem_limit_bytes=56 * 2**20
        ),
    )(embeddings, clusters.reshape(1, rows), doc_order.reshape(1, rows))
    return out.reshape(rows)


def solution(mesh):
    in_specs = (P(("dp", "help"), None), P(("dp", "help")), P(("dp", "help")))
    out_specs = P(("dp", "help"))
    return jax.shard_map(
        per_device, mesh=mesh, in_specs=in_specs, out_specs=out_specs, check_vma=False
    )
```
